256 devices in a mesh: head: 4 (over z_lo), blk: 64 (over x, z_hi, y, core).
Axes of the slice: x: 4, y: 4, z: 8 (z_hi: 2, z_lo: 4; z = z_hi * 4 + z_lo), core: 2. Of those that a mesh axis runs over, the one named last changes fastest.
Arguments:
- queries: bfloat16 [16384, 2048], P(('blk', 'head')), may hold values from -30 to 30
- keys: bfloat16 [16384, 256], P(('blk', 'head')), may hold values from -30 to 30
- values: bfloat16 [16384, 256], P(('blk', 'head')), may hold values from -6 to 6
- outputs: bfloat16 [16384, 2048], P(('blk', 'head')), may hold values from -6 to 6
- out_grad: bfloat16 [16384, 2048], P(('blk', 'head')), may hold values from -6 to 6
- order: int32 [128], replicated, may hold values from 0 to 127, as said below
Outputs:
- query_grad: bfloat16 [16384, 2048], P(('blk', 'head'))
- key_grad: bfloat16 [16384, 256], P(('blk', 'head'))
- value_grad: bfloat16 [16384, 256], P(('blk', 'head'))
The draws below stay inside these ranges and needn't reach their ends.
Inputs may be any that keep to these rules, and one draw needn't show every extreme that they name: Layout block p holds rows p * 128 to (p + 1) * 128 - 1 and the tokens of sequence block order[p]; for every p < 64, order[2 * p] = m and order[2 * p + 1] = 127 - m, where the m of the pairs run over a permutation of 0 to 63.
All inputs are finite; a program needn't handle non-finite values.
Results may differ from the reference program's by a relative error of at most 0.017.
Values may be sent and summed in bfloat16 or wider, within the bound.
No kernel may reach another device: no remote copies, remote signals or barrier semaphores. Data moves between devices by JAX's collectives and lax.ppermute only.
A program may use at most 64 MiB of HBM per device.

```python
import jax
import jax.numpy as jnp
from jax import lax

HEADS = 16
KV_HEADS = 2
HEAD_DIM = 128
SEQ = 16384
BLOCK = 128
BLOCKS = 128


def layout_plan(key):
    half_count = BLOCKS // 2
    relabel = jax.random.permutation(jax.random.fold_in(key, 91), half_count).astype(jnp.int32)
    paired = jnp.stack([relabel, BLOCKS - 1 - relabel], axis=1)
    return paired.reshape(BLOCKS).astype(jnp.int32)


def draw_order(key, part):
    return layout_plan(key)


def draw_queries(key, part):
    key = jax.random.fold_in(key, 1)
    drawn = jax.random.truncated_normal(key, -6.0, 6.0, (SEQ, HEADS, HEAD_DIM), jnp.float32)
    return drawn.reshape(SEQ, HEADS * HEAD_DIM).astype(jnp.bfloat16)


def draw_keys(key, part):
    key = jax.random.fold_in(key, 3)
    drawn = jax.random.truncated_normal(key, -6.0, 6.0, (SEQ, KV_HEADS, HEAD_DIM), jnp.float32)
    return drawn.reshape(SEQ, KV_HEADS * HEAD_DIM).astype(jnp.bfloat16)


def block_levels(own_key, shape, cuts, least, top_value):
    loudness = 1.0
    for dim, parts in cuts:
        steps = jax.random.uniform(jax.random.fold_in(jax.random.fold_in(own_key, 6), dim), (parts,), jnp.float32, least / len(cuts), top_value / len(cuts))
        loudness = loudness * jnp.repeat(jnp.exp(steps), shape[dim] // parts).reshape((-1,) + (1,) * (len(shape) - 1 - dim))
    return loudness


def centred(own_key, dims, scale, reach, cuts=(), kind=jnp.bfloat16):
    result = jax.random.normal(own_key, dims, jnp.float32) * scale
    if len(cuts) > 0:
        result = block_levels(own_key, dims, cuts, -0.22, 0.18) * result
    return jnp.clip(result, min=-reach, max=reach).astype(kind)


def setup_inputs(seed: int = 0) -> dict:
    key_of = jax.random.split(jax.random.key(seed), 7)
    queries = draw_queries(jax.random.fold_in(key_of[6], 71), 0)
    keys = draw_keys(jax.random.fold_in(key_of[6], 71), 0)
    values = centred(key_of[2], (SEQ, KV_HEADS * HEAD_DIM), 1.0, 6.0, ((0, 256),))
    outputs = centred(key_of[3], (SEQ, HEADS * HEAD_DIM), 1.0, 6.0, ((0, 256),))
    out_grad = centred(key_of[4], (SEQ, HEADS * HEAD_DIM), 1.0, 6.0, ((0, 256),))
    order = draw_order(jax.random.fold_in(key_of[6], 71), 0)
    return {"queries": queries, "keys": keys, "values": values, "outputs": outputs, "out_grad": out_grad, "order": order}


def reference(queries, keys, values, outputs, out_grad, order):
    group_size = HEADS // KV_HEADS
    factor = HEAD_DIM ** -0.5
    inverse = jnp.zeros((BLOCKS,), jnp.int32).at[order].set(jnp.arange(BLOCKS, dtype=jnp.int32))

    def to_sequence(matrix, heads_here):
        return matrix.reshape(BLOCKS, BLOCK, -1)[inverse].reshape(BLOCKS, BLOCK, KV_HEADS, heads_here, HEAD_DIM)

    query_seq = to_sequence(queries, group_size)
    out_seq = to_sequence(outputs, group_size)
    grad_seq = to_sequence(out_grad, group_size)
    key_seq = to_sequence(keys, 1)[:, :, :, 0]
    value_seq = to_sequence(values, 1)[:, :, :, 0]
    lower_mask = jnp.arange(BLOCK)[None, :] <= jnp.arange(BLOCK)[:, None]

    def scores_of(query_block, key_block, diagonal):
        scores = jnp.einsum("tkgd,skd->kgts", query_block.astype(jnp.float32), key_block.astype(jnp.float32)) * factor
        valid_mask = jnp.logical_or(jnp.logical_not(diagonal), lower_mask)[None, None]
        return scores, valid_mask

    def block_lse(query_index):
        query_block = query_seq[query_index]

        def visit_keys(key_index, loop_state):
            def update(loop_state):
                running_max, running_sum = loop_state
                scores, valid_mask = scores_of(query_block, key_seq[key_index], key_index == query_index)
                new_max = jnp.maximum(running_max, jnp.max(jnp.where(valid_mask, scores, -1e30), axis=-1))
                running_sum = running_sum * jnp.exp(running_max - new_max) + jnp.sum(
                    jnp.where(valid_mask, jnp.exp(scores - new_max[..., None]), 0.0), axis=-1)
                return new_max, running_sum

            return lax.cond(key_index <= query_index, update, lambda unchanged: unchanged, loop_state)

        start_state = (jnp.full((KV_HEADS, group_size, BLOCK), -1e30, jnp.float32),
                       jnp.zeros((KV_HEADS, group_size, BLOCK), jnp.float32))
        running_max, running_sum = lax.fori_loop(0, BLOCKS, visit_keys, start_state)
        return running_max + jnp.log(running_sum)

    lse = lax.map(block_lse, jnp.arange(BLOCKS, dtype=jnp.int32))
    row_delta = jnp.sum(grad_seq.astype(jnp.float32) * out_seq.astype(jnp.float32), axis=-1).transpose(0, 2, 3, 1)

    def key_step(key_index, loop_state):
        query_acc, key_acc, value_acc = loop_state
        key_block = key_seq[key_index]
        value_block = value_seq[key_index]

        def query_step(query_index, inner_state):
            def tile_grads(inner_state):
                query_acc, key_part, value_part = inner_state
                query_block = query_seq[query_index]
                grad_block = grad_seq[query_index]
                scores, valid_mask = scores_of(query_block, key_block, key_index == query_index)
                weights = jnp.where(valid_mask, jnp.exp(scores - lse[query_index][..., None]), 0.0)
                weights_b = weights.astype(jnp.bfloat16)
                value_part = value_part + jnp.einsum("kgts,tkgd->skd", weights_b.astype(jnp.float32), grad_block.astype(jnp.float32))
                dprob = jnp.einsum("tkgd,skd->kgts", grad_block.astype(jnp.float32), value_block.astype(jnp.float32))
                score_grad = (weights * (dprob - row_delta[query_index][..., None]) * factor).astype(jnp.bfloat16)
                query_acc = query_acc.at[query_index].add(
                    jnp.einsum("kgts,skd->tkgd", score_grad.astype(jnp.float32), key_block.astype(jnp.float32)))
                key_part = key_part + jnp.einsum("kgts,tkgd->skd", score_grad.astype(jnp.float32), query_block.astype(jnp.float32))
                return query_acc, key_part, value_part

            return lax.cond(query_index >= key_index, tile_grads, lambda unchanged: unchanged, inner_state)

        zero_part = jnp.zeros((BLOCK, KV_HEADS, HEAD_DIM), jnp.float32)
        query_acc, key_part, value_part = lax.fori_loop(0, BLOCKS, query_step, (query_acc, zero_part, zero_part))
        return query_acc, key_acc.at[key_index].set(key_part), value_acc.at[key_index].set(value_part)

    start_state = (jnp.zeros((BLOCKS, BLOCK, KV_HEADS, group_size, HEAD_DIM), jnp.float32),
                   jnp.zeros((BLOCKS, BLOCK, KV_HEADS, HEAD_DIM), jnp.float32),
                   jnp.zeros((BLOCKS, BLOCK, KV_HEADS, HEAD_DIM), jnp.float32))
    query_acc, key_acc, value_acc = lax.fori_loop(0, BLOCKS, key_step, start_state)
    query_grad = query_acc.astype(jnp.bfloat16).reshape(BLOCKS, BLOCK, HEADS * HEAD_DIM)[order].reshape(SEQ, HEADS * HEAD_DIM)
    key_grad = key_acc.astype(jnp.bfloat16).reshape(BLOCKS, BLOCK, KV_HEADS * HEAD_DIM)[order].reshape(SEQ, KV_HEADS * HEAD_DIM)
    value_grad = value_acc.astype(jnp.bfloat16).reshape(BLOCKS, BLOCK, KV_HEADS * HEAD_DIM)[order].reshape(SEQ, KV_HEADS * HEAD_DIM)
    return query_grad, key_grad, value_grad
```

```python
from functools import partial
import math

import jax
import jax.numpy as jnp
from jax import lax
from jax.experimental import pallas as pl
from jax.experimental.pallas import tpu as pltpu
from jax.sharding import Mesh, PartitionSpec as P

HEAD_DIM = 128
BLOCK = 128
HEADS_HERE = 4
ROWS = BLOCK * HEADS_HERE
CHUNK_BLOCKS = 4
CHUNK = CHUNK_BLOCKS * BLOCK
SLOTS = 64
CHUNKS = SLOTS // CHUNK_BLOCKS
PIECE = 2048
FACTOR = HEAD_DIM ** (-0.5)
LOG2E = math.log2(math.e)
SCALE2 = FACTOR * LOG2E
NEG = -1e30
VMEM_BYTES = 48 * 1024 * 1024
PIECE_ROWS = (PIECE, PIECE, PIECE, PIECE // 2, PIECE // 2)
PIECE_START = (0, PIECE, 2 * PIECE, 3 * PIECE, 3 * PIECE + PIECE // 2)


def ring_pairs(steps):
    return [(source, (source + steps) % 4) for source in range(4)]


def send(value, axis, steps):
    return lax.ppermute(value, axis, ring_pairs(steps))


def swap_core(value):
    return lax.ppermute(value, "core", [(0, 1), (1, 0)])


def gather_ring(own, axis):
    half = own.shape[0] // 2
    left = send(own, axis, 1)
    right = send(own, axis, -1)
    far_first = send(left[:half], axis, 1)
    far_second = send(right[half:], axis, -1)
    return [own, left, right, far_first, far_second]


def add(first, second):
    return (first.astype(jnp.float32) + second.astype(jnp.float32)).astype(jnp.bfloat16)


def reduce_ring(pieces, axis):
    own, left, right, far_first, far_second = pieces
    half = own.shape[0] // 2
    from_right = send(far_first, axis, -1)
    from_left = send(far_second, axis, 1)
    left = jnp.concatenate([add(left[:half], from_right), left[half:]], axis=0)
    right = jnp.concatenate([right[:half], add(right[half:], from_left)], axis=0)
    first = send(left, axis, -1)
    second = send(right, axis, 1)
    return (
        own.astype(jnp.float32) + first.astype(jnp.float32) + second.astype(jnp.float32)
    ).astype(jnp.bfloat16)


def split_pieces(rows):
    step = rows.shape[0] // 4
    half = step // 2
    return [
        rows[:step],
        rows[step : 2 * step],
        rows[2 * step : 3 * step],
        rows[3 * step : 3 * step + half],
        rows[3 * step + half :],
    ]


def copy_pieces(sources, target, sems):
    copies = []
    for index, source in enumerate(sources):
        copy = pltpu.make_async_copy(
            source, target.at[pl.ds(PIECE_START[index], PIECE_ROWS[index])], sems.at[index]
        )
        copy.start()
        copies.append(copy)
    return copies


def spread_heads(source, base, target):
    for pair in range(2):
        for head in range(HEADS_HERE):
            target[base + pair, pl.ds(head * BLOCK, BLOCK), :] = source[
                pl.ds(pair * BLOCK, BLOCK), pl.ds(head * HEAD_DIM, HEAD_DIM)
            ]


def load_chunk(source, slot_ref, chunk):
    return jnp.concatenate(
        [
            source[pl.ds(pl.multiple_of(slot_ref[chunk * CHUNK_BLOCKS + j] * BLOCK, BLOCK), BLOCK), :]
            for j in range(CHUNK_BLOCKS)
        ],
        axis=0,
    )


def dot_rows(left, right):
    return lax.dot_general(
        left, right, (((1,), (1,)), ((), ())), preferred_element_type=jnp.float32
    )


def dot_columns(left, right):
    return lax.dot_general(
        left, right, (((0,), (0,)), ((), ())), preferred_element_type=jnp.float32
    )


def masked(value, fill, ids_ref, chunk, query_id):
    rows = lax.broadcasted_iota(jnp.int32, (BLOCK, ROWS), 0)
    lanes = lax.broadcasted_iota(jnp.int32, (BLOCK, ROWS), 1) % BLOCK
    ahead = rows - lanes
    parts = []
    for j in range(CHUNK_BLOCKS):
        limit = (query_id - ids_ref[chunk * CHUNK_BLOCKS + j]) * BLOCK
        parts.append(jnp.where(ahead <= limit, value[j * BLOCK : (j + 1) * BLOCK], fill))
    return jnp.concatenate(parts, axis=0)


def for_tiles(chunk, query, count_ref, tile):
    count = count_ref[query]
    full = count // CHUNK_BLOCKS

    @pl.when(chunk < full)
    def _():
        tile(chunk, query, False)

    @pl.when((chunk >= full) & (chunk * CHUNK_BLOCKS < count_ref[query + 4]))
    def _():
        tile(chunk, query, True)


def lse_kernel(
    slot_ref, ids_ref, count_ref, qid_ref, q_own, q_other, k0, k1, k2, k3, k4,
    max_ref, sum_ref, keys, queries, max_acc, sum_acc, sems,
):
    copies = copy_pieces((k0, k1, k2, k3, k4), keys, sems)
    spread_heads(q_own, 0, queries)
    spread_heads(q_other, 2, queries)
    max_acc[...] = jnp.full(max_acc.shape, NEG, jnp.float32)
    sum_acc[...] = jnp.zeros(sum_acc.shape, jnp.float32)
    for copy in copies:
        copy.wait()

    def tile(chunk, query, use_mask):
        scores = dot_rows(load_chunk(keys, slot_ref, chunk), queries[query])
        if use_mask:
            scores = masked(scores, NEG, ids_ref, chunk, qid_ref[query])
        grouped = scores.reshape(CHUNK // 8, 8, ROWS)
        old_max = max_acc[query]
        new_max = jnp.maximum(old_max, jnp.max(grouped, axis=0))
        weights = jnp.exp2((grouped - new_max[None]) * SCALE2)
        sum_acc[query] = sum_acc[query] * jnp.exp2((old_max - new_max) * SCALE2) + jnp.sum(
            weights, axis=0
        )
        max_acc[query] = new_max

    def step(index, carry):
        for_tiles(index // 4, index % 4, count_ref, tile)
        return carry

    lax.fori_loop(0, CHUNKS * 4, step, 0)
    for query in range(4):
        part_max = max_acc[query]
        top = jnp.max(part_max, axis=0, keepdims=True)
        max_ref[query] = top
        sum_ref[query] = jnp.sum(
            sum_acc[query] * jnp.exp2((part_max - top) * SCALE2), axis=0, keepdims=True
        )


def grad_kernel(
    slot_k_ref, slot_v_ref, ids_ref, count_ref, qid_ref,
    q_own, q_other, g_own, g_other, max_mine, sum_mine, max_theirs, sum_theirs,
    delta_own, delta_other,
    k0, k1, k2, k3, k4, v0, v1, v2, v3, v4,
    dq_own, dq_other, dk0, dk1, dk2, dk3, dk4, dv0, dv1, dv2, dv3, dv4,
    keys, values, queries, grads, lse, delta, dk_all, dv_all, dk_acc, dv_acc, dq_acc,
    sems_k, sems_v,
):
    copies = copy_pieces((k0, k1, k2, k3, k4), keys, sems_k)
    copies += copy_pieces((v0, v1, v2, v3, v4), values, sems_v)
    spread_heads(q_own, 0, queries)
    spread_heads(q_other, 2, queries)
    spread_heads(g_own, 0, grads)
    spread_heads(g_other, 2, grads)
    for query in range(4):
        top_mine = max_mine[query]
        top_theirs = max_theirs[(query + 2) % 4]
        top = jnp.maximum(top_mine, top_theirs)
        total = sum_mine[query] * jnp.exp2((top_mine - top) * SCALE2) + sum_theirs[
            (query + 2) % 4
        ] * jnp.exp2((top_theirs - top) * SCALE2)
        lse[query] = top * SCALE2 + jnp.log2(total)
        delta[query] = (delta_own if query < 2 else delta_other)[query % 2]
    dq_acc[...] = jnp.zeros(dq_acc.shape, jnp.float32)
    for copy in copies:
        copy.wait()

    def tile(chunk, query, use_mask):
        key_part = load_chunk(keys, slot_k_ref, chunk)
        value_part = load_chunk(values, slot_v_ref, chunk)
        query_part = queries[query]
        grad_part = grads[query]
        scores = dot_rows(key_part, query_part)
        weights = jnp.exp2(scores * SCALE2 - lse[query])
        if use_mask:
            weights = masked(weights, 0.0, ids_ref, chunk, qid_ref[query])
        dv_acc[...] += jnp.dot(
            weights.astype(jnp.bfloat16), grad_part, preferred_element_type=jnp.float32
        )
        dprob = dot_rows(value_part, grad_part)
        score_grad = (weights * (dprob - delta[query])).astype(jnp.bfloat16)
        dk_acc[...] += jnp.dot(score_grad, query_part, preferred_element_type=jnp.float32)
        dq_acc[query] += dot_columns(key_part, score_grad)

    def chunk_step(chunk, carry):
        dk_acc[...] = jnp.zeros(dk_acc.shape, jnp.float32)
        dv_acc[...] = jnp.zeros(dv_acc.shape, jnp.float32)

        def query_step(query, inner):
            for_tiles(chunk, query, count_ref, tile)
            return inner

        lax.fori_loop(0, 4, query_step, 0)
        for j in range(CHUNK_BLOCKS):
            place = chunk * CHUNK_BLOCKS + j
            rows = pl.ds(j * BLOCK, BLOCK)
            start_k = pl.multiple_of(slot_k_ref[place] * BLOCK, BLOCK)
            start_v = pl.multiple_of(slot_v_ref[place] * BLOCK, BLOCK)
            dk_all[pl.ds(start_k, BLOCK), :] = (dk_acc[rows, :] * FACTOR).astype(jnp.bfloat16)
            dv_all[pl.ds(start_v, BLOCK), :] = dv_acc[rows, :].astype(jnp.bfloat16)
        return carry

    lax.fori_loop(0, CHUNKS, chunk_step, 0)
    outs = []
    for source, targets, sems in (
        (dk_all, (dk0, dk1, dk2, dk3, dk4), sems_k),
        (dv_all, (dv0, dv1, dv2, dv3, dv4), sems_v),
    ):
        for index, target in enumerate(targets):
            copy = pltpu.make_async_copy(
                source.at[pl.ds(PIECE_START[index], PIECE_ROWS[index])], target, sems.at[index]
            )
            copy.start()
            outs.append(copy)
    for query in range(4):
        target = dq_own if query < 2 else dq_other
        for head in range(HEADS_HERE):
            part = dq_acc[query, :, pl.ds(head * BLOCK, BLOCK)] * FACTOR
            target[pl.ds((query % 2) * BLOCK, BLOCK), pl.ds(head * HEAD_DIM, HEAD_DIM)] = (
                part.T.astype(target.dtype)
            )
    for copy in outs:
        copy.wait()


SMEM = pl.BlockSpec(memory_space=pltpu.SMEM)
VMEM = pl.BlockSpec(memory_space=pltpu.VMEM)
ANY = pl.BlockSpec(memory_space=pl.ANY)
PAIRS = SLOTS * 2 + 1


def call_lse(slots, ids, counts, qids, q_own, q_other, key_pieces):
    stat = jax.ShapeDtypeStruct((4, 1, ROWS), jnp.float32)
    work = PAIRS * BLOCK * ROWS
    return pl.pallas_call(
        lse_kernel,
        out_shape=(stat, stat),
        in_specs=[SMEM] * 4 + [VMEM] * 2 + [ANY] * 5,
        out_specs=(VMEM, VMEM),
        scratch_shapes=[
            pltpu.VMEM((SLOTS * BLOCK, HEAD_DIM), jnp.bfloat16),
            pltpu.VMEM((4, ROWS, HEAD_DIM), jnp.bfloat16),
            pltpu.VMEM((4, 8, ROWS), jnp.float32),
            pltpu.VMEM((4, 8, ROWS), jnp.float32),
            pltpu.SemaphoreType.DMA((5,)),
        ],
        compiler_params=pltpu.CompilerParams(vmem_limit_bytes=VMEM_BYTES),
        cost_estimate=pl.CostEstimate(
            flops=8 * work * HEAD_DIM, bytes_accessed=3 << 20, transcendentals=work
        ),
        name="lse",
    )(slots, ids, counts, qids, q_own, q_other, *key_pieces)


def call_grads(tables, rows, key_pieces, value_pieces):
    pieces = tuple(jax.ShapeDtypeStruct((n, HEAD_DIM), jnp.bfloat16) for n in PIECE_ROWS)
    work = PAIRS * BLOCK * ROWS
    flat = jax.ShapeDtypeStruct((2 * BLOCK, ROWS), jnp.float32)
    return pl.pallas_call(
        grad_kernel,
        out_shape=(flat, jax.ShapeDtypeStruct(flat.shape, jnp.bfloat16)) + pieces + pieces,
        in_specs=[SMEM] * 5 + [VMEM] * 10 + [ANY] * 10,
        out_specs=(VMEM, VMEM) + (ANY,) * 10,
        scratch_shapes=[
            pltpu.VMEM((SLOTS * BLOCK, HEAD_DIM), jnp.bfloat16),
            pltpu.VMEM((SLOTS * BLOCK, HEAD_DIM), jnp.bfloat16),
            pltpu.VMEM((4, ROWS, HEAD_DIM), jnp.bfloat16),
            pltpu.VMEM((4, ROWS, HEAD_DIM), jnp.bfloat16),
            pltpu.VMEM((4, 1, ROWS), jnp.float32),
            pltpu.VMEM((4, 1, ROWS), jnp.float32),
            pltpu.VMEM((SLOTS * BLOCK, HEAD_DIM), jnp.bfloat16),
            pltpu.VMEM((SLOTS * BLOCK, HEAD_DIM), jnp.bfloat16),
            pltpu.VMEM((CHUNK, HEAD_DIM), jnp.float32),
            pltpu.VMEM((CHUNK, HEAD_DIM), jnp.float32),
            pltpu.VMEM((4, HEAD_DIM, ROWS), jnp.float32),
            pltpu.SemaphoreType.DMA((5,)),
            pltpu.SemaphoreType.DMA((5,)),
        ],
        compiler_params=pltpu.CompilerParams(vmem_limit_bytes=VMEM_BYTES),
        cost_estimate=pl.CostEstimate(
            flops=16 * work * HEAD_DIM, bytes_accessed=10 << 20, transcendentals=work
        ),
        name="grads",
    )(*tables, *rows, *key_pieces, *value_pieces)


def lookup(table, wanted):
    places = jnp.arange(table.shape[0], dtype=jnp.int32)
    return jnp.sum(jnp.where(wanted[:, None] == places[None, :], table[None, :], 0), axis=1)


def plan(order):
    x, y, zh, core = (lax.axis_index(name) for name in ("x", "y", "zh", "core"))
    offsets = (0, -1, 1, 2)
    offset_table = jnp.array(offsets, jnp.int32)
    slot = jnp.arange(SLOTS, dtype=jnp.int32)
    outer, inner, pair = slot // 16, slot // 4 % 4, slot % 4

    def block_of(dx, dy):
        blk = ((x + dx) % 4) * 16 + (pair // 2) * 8 + ((y + dy) % 4) * 2 + core
        return lookup(order, 2 * blk + pair % 2)

    outer, inner = lookup(offset_table, outer), lookup(offset_table, inner)
    ids_k, ids_v = block_of(outer, inner), block_of(inner, outer)
    own = ((x * 2 + zh) * 4 + y) * 2 + core
    other = own + 1 - 2 * core
    ends = jnp.arange(2, dtype=jnp.int32)
    query_ids = lookup(order, jnp.concatenate([2 * own + ends, 2 * other + ends]))

    def in_sequence(ids):
        rank = jnp.sum((ids[None, :] < ids[:, None]).astype(jnp.int32), axis=1)
        hit = rank[None, :] == slot[:, None]
        return (
            jnp.sum(jnp.where(hit, slot[None, :], 0), axis=1),
            jnp.sum(jnp.where(hit, ids[None, :], 0), axis=1),
        )

    slots_k, ids = in_sequence(ids_k)
    slots_v, _ = in_sequence(ids_v)
    before = jnp.sum((ids[None, :] < query_ids[:, None]).astype(jnp.int32), axis=1)
    upto = jnp.sum((ids[None, :] <= query_ids[:, None]).astype(jnp.int32), axis=1)
    return slots_k, slots_v, ids, jnp.concatenate([before, upto]), query_ids


def to_heads(rows):
    parts = rows.reshape(rows.shape[0], 4, -1).transpose(1, 0, 2)
    parts = lax.all_to_all(parts, "head", split_axis=0, concat_axis=0, tiled=True)
    return parts.reshape(4 * rows.shape[0], -1)


def body(queries, keys, values, outputs, out_grad, order):
    tokens = queries.shape[0]
    slots_k, slots_v, ids, counts, query_ids = plan(order)

    both = jnp.stack(
        [keys.reshape(tokens, 2, HEAD_DIM), values.reshape(tokens, 2, HEAD_DIM)], axis=0
    ).transpose(2, 0, 1, 3)
    outgoing = jnp.broadcast_to(
        both[None, :, None], (2, 2, 2) + both.shape[1:]
    ).reshape(8, 2, tokens, HEAD_DIM)
    arrived = lax.all_to_all(outgoing, ("zh", "head"), split_axis=0, concat_axis=0, tiled=True)
    key_pieces = gather_ring(
        jnp.concatenate(gather_ring(arrived[:, 0].reshape(8 * tokens, HEAD_DIM), "y")), "x"
    )
    value_pieces = gather_ring(
        jnp.concatenate(gather_ring(arrived[:, 1].reshape(8 * tokens, HEAD_DIM), "x")), "y"
    )

    q_own = to_heads(queries)
    g_own = to_heads(out_grad)
    row_delta = jnp.sum(
        (out_grad.astype(jnp.float32) * outputs.astype(jnp.float32)).reshape(tokens, 16, HEAD_DIM),
        axis=2,
    )
    delta = lax.all_to_all(
        row_delta.T.reshape(4, 4, tokens), "head", split_axis=0, concat_axis=0, tiled=True
    )
    delta_own = delta.reshape(2, 2, 4, tokens).transpose(0, 2, 1, 3).reshape(2, 1, ROWS)
    q_other, g_other, delta_other = swap_core(q_own), swap_core(g_own), swap_core(delta_own)

    max_mine, sum_mine = call_lse(slots_k, ids, counts, query_ids, q_own, q_other, key_pieces)
    max_theirs, sum_theirs = swap_core(max_mine), swap_core(sum_mine)
    results = call_grads(
        (slots_k, slots_v, ids, counts, query_ids),
        (
            q_own, q_other, g_own, g_other, max_mine, sum_mine, max_theirs, sum_theirs,
            delta_own, delta_other,
        ),
        key_pieces,
        value_pieces,
    )
    dq_own, dq_other = results[0], results[1]
    dq = (dq_own + swap_core(dq_other).astype(jnp.float32)).astype(jnp.bfloat16)
    dq = lax.all_to_all(
        dq.reshape(4, tokens, ROWS), "head", split_axis=0, concat_axis=0, tiled=True
    )
    query_grad = dq.transpose(1, 0, 2).reshape(tokens, 4 * ROWS)

    dk = reduce_ring(split_pieces(reduce_ring(results[2:7], "x")), "y")
    dv = reduce_ring(split_pieces(reduce_ring(results[7:12], "y")), "x")
    back = jnp.stack(
        [dk.reshape(8, tokens, HEAD_DIM), dv.reshape(8, tokens, HEAD_DIM)], axis=1
    )
    back = lax.all_to_all(back, ("zh", "head"), split_axis=0, concat_axis=0, tiled=True)
    summed = jnp.sum(
        back.reshape(2, 2, 2, 2, tokens, HEAD_DIM).astype(jnp.float32), axis=(0, 2)
    )
    folded = summed.transpose(1, 2, 0, 3).reshape(2, tokens, 2 * HEAD_DIM).astype(jnp.bfloat16)
    return query_grad, folded[0], folded[1]


def solution(mesh):
    fine = Mesh(
        mesh.devices.reshape(4, 4, 2, 4, 2), ("head", "x", "zh", "y", "core")
    )
    rows = P(("x", "zh", "y", "core", "head"), None)
    return jax.shard_map(
        body,
        mesh=fine,
        in_specs=(rows, rows, rows, rows, rows, P()),
        out_specs=(rows, rows, rows),
        check_vma=False,
    )
```

```python
from functools import partial
import math

import jax
import jax.numpy as jnp
from jax import lax
from jax.experimental import pallas as pl
from jax.experimental.pallas import tpu as pltpu
from jax.sharding import Mesh, PartitionSpec as P

HEAD_DIM = 128
BLOCK = 128
TOKENS = 64
HEADS_HERE = 8
ROWS = TOKENS * HEADS_HERE
WIDE = HEADS_HERE * HEAD_DIM
CHUNK_BLOCKS = 4
CHUNK = CHUNK_BLOCKS * BLOCK
SLOTS = 32
TILES = 8
CHUNKS = SLOTS // CHUNK_BLOCKS
PIECE = 512
PIECES = 4
OTHER = PIECES * PIECE
PAIR = 2 * HEAD_DIM
OFFSETS = (0, -1, 1, 2)
PIECE_AT = {offset % 4: index for index, offset in enumerate(OFFSETS)}
FACTOR = HEAD_DIM ** (-0.5)
LOG2E = math.log2(math.e)
SCALE2 = FACTOR * LOG2E
NEG = -1e30
VMEM_BYTES = 48 * 1024 * 1024

def ring_pairs(steps):
    return [(source, (source + steps) % 4) for source in range(4)]


def send(value, axis, steps):
    return lax.ppermute(value, axis, ring_pairs(steps))


def swap_core(value):
    return lax.ppermute(value, "core", [(0, 1), (1, 0)])


def swap_group(value):
    return lax.ppermute(value, "head", [(source, source ^ 2) for source in range(4)])


def swap_half(value):
    return lax.ppermute(value, "head", [(source, source ^ 1) for source in range(4)])


def swap_z(value):
    return lax.ppermute(value, "zh", [(0, 1), (1, 0)])


def swap_both(value):
    return lax.ppermute(value, ("head", "zh"), [(source, source ^ 5) for source in range(8)])


def gather_direct(own, axis):
    return [own] + [send(own, axis, -offset) for offset in OFFSETS[1:]]


def wide(value):
    return value.astype(jnp.float32)


def add(*values):
    total = wide(values[0])
    for value in values[1:]:
        total = total + wide(value)
    return total.astype(jnp.bfloat16)


def reduce_direct(pieces, axis):
    arrived = [send(piece, axis, offset) for piece, offset in zip(pieces[1:], OFFSETS[1:])]
    return add(pieces[0], *arrived)


def kv_copies(pieces, other, gathered, sems, outward):
    copies = []
    for index in range(PIECES + 1):
        outside = other if index == PIECES else pieces[index]
        inside = gathered.at[pl.ds(index * PIECE, outside.shape[0])]
        ends = (inside, outside) if outward else (outside, inside)
        copy = pltpu.make_async_copy(*ends, sems.at[index])
        copy.start()
        copies.append(copy)
    return copies


def spread_heads(sources, target):
    for tile in range(TILES):
        for head in range(HEADS_HERE):
            target[tile, pl.ds(head * TOKENS, TOKENS), :] = sources[tile // 2][
                pl.ds(tile % 2 * TOKENS, TOKENS), pl.ds(head * HEAD_DIM, HEAD_DIM)
            ]


def load_chunk(source, slot_ref, chunk, column):
    return jnp.concatenate(
        [
            source[pl.ds(pl.multiple_of(slot_ref[chunk * CHUNK_BLOCKS + j] * BLOCK, BLOCK), BLOCK),
                pl.ds(column, HEAD_DIM),
            ]
            for j in range(CHUNK_BLOCKS)
        ],
        axis=0,
    )


def dot_rows(left, right):
    return lax.dot_general(
        left, right, (((1,), (1,)), ((), ())), preferred_element_type=jnp.float32
    )


def dot_columns(left, right):
    return lax.dot_general(
        left, right, (((0,), (0,)), ((), ())), preferred_element_type=jnp.float32
    )


def masked(value, fill, ids_ref, chunk, query_start):
    rows = lax.broadcasted_iota(jnp.int32, (BLOCK, ROWS), 0)
    lanes = lax.broadcasted_iota(jnp.int32, (BLOCK, ROWS), 1) % TOKENS
    ahead = rows - lanes
    parts = []
    for j in range(CHUNK_BLOCKS):
        limit = query_start - ids_ref[chunk * CHUNK_BLOCKS + j] * BLOCK
        parts.append(jnp.where(ahead <= limit, value[j * BLOCK : (j + 1) * BLOCK], fill))
    return jnp.concatenate(parts, axis=0)


def for_tiles(chunk, query, count_ref, tile):
    count = count_ref[query]
    full = count // CHUNK_BLOCKS

    @pl.when(chunk < full)
    def _():
        tile(chunk, query, False)

    @pl.when((chunk >= full) & (chunk * CHUNK_BLOCKS < count_ref[query + TILES]))
    def _():
        tile(chunk, query, True)


def lse_kernel(slot_ref, ids_ref, count_ref, start_ref, delta_ref, *refs):
    rows, pieces, other = refs[:4], refs[4 : 4 + PIECES], refs[4 + PIECES]
    stat_ref, gathered, queries, max_acc, sum_acc, sems = refs[5 + PIECES :]
    copies = kv_copies(pieces, other, gathered, sems, False)
    spread_heads(rows, queries)
    max_acc[...] = jnp.full(max_acc.shape, NEG, jnp.float32)
    sum_acc[...] = jnp.zeros(sum_acc.shape, jnp.float32)
    for copy in copies:
        copy.wait()

    def tile(chunk, query, use_mask):
        scores = dot_rows(load_chunk(gathered, slot_ref, chunk, 0), queries[query])
        if use_mask:
            scores = masked(scores, NEG, ids_ref, chunk, start_ref[query])
        grouped = scores.reshape(CHUNK // 8, 8, ROWS)
        old_max = max_acc[query]
        new_max = jnp.maximum(old_max, jnp.max(grouped, axis=0))
        weights = jnp.exp2((grouped - new_max[None]) * SCALE2)
        sum_acc[query] = sum_acc[query] * jnp.exp2((old_max - new_max) * SCALE2) + jnp.sum(
            weights, axis=0
        )
        max_acc[query] = new_max

    def step(index, carry):
        for_tiles(index // TILES, index % TILES, count_ref, tile)
        return carry

    lax.fori_loop(0, CHUNKS * TILES, step, 0)
    for query in range(2):
        stat_ref[2 * TILES + query] = delta_ref[query]
    for query in range(TILES):
        part_max = max_acc[query]
        top = jnp.max(part_max, axis=0, keepdims=True)
        stat_ref[query] = top
        stat_ref[TILES + query] = jnp.sum(
            sum_acc[query] * jnp.exp2((part_max - top) * SCALE2), axis=0, keepdims=True
        )


def grad_kernel(slot_ref, ids_ref, count_ref, start_ref, *refs):
    q_rows, g_rows, stats = refs[:4], refs[4:8], refs[8:12]
    pieces, other = refs[12 : 12 + PIECES], refs[12 + PIECES]
    refs = refs[13 + PIECES :]
    dq_pieces, d_pieces, d_other = refs[:4], refs[4 : 4 + PIECES], refs[4 + PIECES]
    gathered, queries, grads, lse, delta, d_all, dk_acc, dv_acc, dq_acc, sems = refs[5 + PIECES :]
    copies = kv_copies(pieces, other, gathered, sems, False)
    spread_heads(q_rows, queries)
    spread_heads(g_rows, grads)
    for query in range(TILES):
        offset = OFFSETS[query // 2]
        places = [2 * PIECE_AT[(offset - source) % 4] + query % 2 for source in OFFSETS]
        tops = [stat[place] for stat, place in zip(stats, places)]
        top = jnp.maximum(jnp.maximum(tops[0], tops[1]), jnp.maximum(tops[2], tops[3]))
        total = jnp.zeros_like(top)
        for stat, place, part in zip(stats, places, tops):
            total += stat[TILES + place] * jnp.exp2((part - top) * SCALE2)
        lse[query] = top * SCALE2 + jnp.log2(total)
        delta[query] = stats[query // 2][2 * TILES + query % 2]
    dq_acc[...] = jnp.zeros(dq_acc.shape, jnp.float32)
    for copy in copies:
        copy.wait()

    def tile(chunk, query, use_mask):
        key_part = load_chunk(gathered, slot_ref, chunk, 0)
        value_part = load_chunk(gathered, slot_ref, chunk, HEAD_DIM)
        query_part = queries[query]
        grad_part = grads[query]
        scores = dot_rows(key_part, query_part)
        weights = jnp.exp2(scores * SCALE2 - lse[query])
        if use_mask:
            weights = masked(weights, 0.0, ids_ref, chunk, start_ref[query])
        dv_acc[...] += jnp.dot(
            weights.astype(jnp.bfloat16), grad_part, preferred_element_type=jnp.float32
        )
        dprob = dot_rows(value_part, grad_part)
        score_grad = (weights * (dprob - delta[query])).astype(jnp.bfloat16)
        dk_acc[...] += jnp.dot(score_grad, query_part, preferred_element_type=jnp.float32)
        dq_acc[query] += dot_columns(key_part, score_grad)

    def chunk_step(chunk, carry):
        dk_acc[...] = jnp.zeros(dk_acc.shape, jnp.float32)
        dv_acc[...] = jnp.zeros(dv_acc.shape, jnp.float32)

        def query_step(query, inner):
            for_tiles(chunk, query, count_ref, tile)
            return inner

        lax.fori_loop(0, TILES, query_step, 0)
        for j in range(CHUNK_BLOCKS):
            place = chunk * CHUNK_BLOCKS + j
            rows = pl.ds(j * BLOCK, BLOCK)
            target = pl.ds(pl.multiple_of(slot_ref[place] * BLOCK, BLOCK), BLOCK)
            d_all[target, pl.ds(0, HEAD_DIM)] = (dk_acc[rows, :] * FACTOR).astype(jnp.bfloat16)
            d_all[target, pl.ds(HEAD_DIM, HEAD_DIM)] = dv_acc[rows, :].astype(jnp.bfloat16)
        return carry

    lax.fori_loop(0, CHUNKS, chunk_step, 0)
    outs = kv_copies(d_pieces, d_other, d_all, sems, True)
    for query in range(TILES):
        target = dq_pieces[query // 2]
        for head in range(0, HEADS_HERE, 2):
            pair = (dq_acc[query, :, pl.ds(head * TOKENS, 2 * TOKENS)] * FACTOR).T
            for half in range(2):
                target[
                    pl.ds((query % 2) * TOKENS, TOKENS),
                    pl.ds((head + half) * HEAD_DIM, HEAD_DIM),
                ] = pair[half * TOKENS : (half + 1) * TOKENS].astype(target.dtype)
    for copy in outs:
        copy.wait()


SMEM = pl.BlockSpec(memory_space=pltpu.SMEM)
VMEM = pl.BlockSpec(memory_space=pltpu.VMEM)
ANY = pl.BlockSpec(memory_space=pl.ANY)
PAIRS = (SLOTS + 2) * TILES // 2


def call_lse(tables, delta, rows, pieces):
    work = PAIRS * BLOCK * ROWS
    return pl.pallas_call(
        lse_kernel,
        out_shape=jax.ShapeDtypeStruct((2 * TILES + 2, 1, ROWS), jnp.float32),
        in_specs=[SMEM] * 4 + [VMEM] * 5 + [ANY] * (PIECES + 1),
        out_specs=VMEM,
        scratch_shapes=[
            pltpu.VMEM((SLOTS * BLOCK, PAIR), jnp.bfloat16),
            pltpu.VMEM((TILES, ROWS, HEAD_DIM), jnp.bfloat16),
            pltpu.VMEM((TILES, 8, ROWS), jnp.float32),
            pltpu.VMEM((TILES, 8, ROWS), jnp.float32),
            pltpu.SemaphoreType.DMA((PIECES + 1,)),
        ],
        compiler_params=pltpu.CompilerParams(vmem_limit_bytes=VMEM_BYTES),
        cost_estimate=pl.CostEstimate(
            flops=8 * work * HEAD_DIM, bytes_accessed=4 << 20, transcendentals=work
        ),
        name="lse",
    )(*tables, delta, *rows, *pieces)


def call_grads(tables, q_rows, g_rows, stats, pieces):
    work = PAIRS * BLOCK * ROWS
    flat = jax.ShapeDtypeStruct((2 * TOKENS, WIDE), jnp.bfloat16)
    piece = jax.ShapeDtypeStruct((PIECE, PAIR), jnp.bfloat16)
    other = jax.ShapeDtypeStruct((OTHER, PAIR), jnp.bfloat16)
    results = pl.pallas_call(
        grad_kernel,
        out_shape=(flat,) * 4 + (piece,) * PIECES + (other,),
        in_specs=[SMEM] * 4 + [VMEM] * 12 + [ANY] * (PIECES + 1),
        out_specs=(VMEM,) * 4 + (ANY,) * (PIECES + 1),
        scratch_shapes=[
            pltpu.VMEM((SLOTS * BLOCK, PAIR), jnp.bfloat16),
            pltpu.VMEM((TILES, ROWS, HEAD_DIM), jnp.bfloat16),
            pltpu.VMEM((TILES, ROWS, HEAD_DIM), jnp.bfloat16),
            pltpu.VMEM((TILES, 1, ROWS), jnp.float32),
            pltpu.VMEM((TILES, 1, ROWS), jnp.float32),
            pltpu.VMEM((SLOTS * BLOCK, PAIR), jnp.bfloat16),
            pltpu.VMEM((CHUNK, HEAD_DIM), jnp.float32),
            pltpu.VMEM((CHUNK, HEAD_DIM), jnp.float32),
            pltpu.VMEM((TILES, HEAD_DIM, ROWS), jnp.float32),
            pltpu.SemaphoreType.DMA((PIECES + 1,)),
        ],
        compiler_params=pltpu.CompilerParams(vmem_limit_bytes=VMEM_BYTES),
        cost_estimate=pl.CostEstimate(
            flops=16 * work * HEAD_DIM, bytes_accessed=8 << 20, transcendentals=work
        ),
        name="grads",
    )(*tables, *q_rows, *g_rows, *stats, *pieces)
    return results[:4], results[4 : 4 + PIECES], results[4 + PIECES]


def lookup(table, wanted):
    places = jnp.arange(table.shape[0], dtype=jnp.int32)
    return jnp.sum(jnp.where(wanted[:, None] == places[None, :], table[None, :], 0), axis=1)


def plan(order):
    x, y, zh, core, head = (lax.axis_index(name) for name in ("x", "y", "zh", "core", "head"))
    group, half = head // 2, head % 2
    offsets = jnp.array(OFFSETS, jnp.int32)
    slot = jnp.arange(SLOTS, dtype=jnp.int32)
    piece, pair = slot // 4 % 4, slot % 4
    blk = (
        x * 16
        + (zh + pair // 2) % 2 * 8
        + (y + lookup(offsets, piece)) % 4 * 2
        + (core + slot // 16) % 2
    )
    ids = lookup(order, 2 * blk + (group + pair) % 2)
    tile = jnp.arange(TILES, dtype=jnp.int32)
    blk = (x + lookup(offsets, tile // 2)) % 4 * 16 + zh * 8 + y * 2 + core
    query_ids = lookup(order, 2 * blk + (group + tile) % 2)
    before = jnp.sum((ids[None, :] < query_ids[:, None]).astype(jnp.int32), axis=1)
    upto = jnp.sum((ids[None, :] <= query_ids[:, None]).astype(jnp.int32), axis=1)
    rank = jnp.sum((ids[None, :] < ids[:, None]).astype(jnp.int32), axis=1)
    hit = rank[None, :] == slot[:, None]
    slots = jnp.sum(jnp.where(hit, slot[None, :], 0), axis=1)
    sorted_ids = jnp.sum(jnp.where(hit, ids[None, :], 0), axis=1)
    counts = jnp.concatenate([before, upto])
    return slots, sorted_ids, counts, query_ids * BLOCK + half * TOKENS


def choose(first, second, swap):
    return jnp.where(swap, second, first), jnp.where(swap, first, second)


def columns(rows, group):
    width = rows.shape[1] // 2
    return choose(rows[:, :width], rows[:, width:], group == 1)


def body(queries, keys, values, outputs, out_grad, order):
    head = lax.axis_index("head")
    group, half = head // 2, head % 2
    tables = plan(order)

    my_keys, their_keys = columns(keys, group)
    my_values, their_values = columns(values, group)
    mine = jnp.concatenate([my_keys, my_values], axis=1)
    theirs = jnp.concatenate([their_keys, their_values], axis=1)
    near = jnp.stack([mine, swap_group(theirs), swap_z(mine), swap_both(theirs)])
    blocks = jnp.concatenate(choose(near, swap_half(near), half == 1), axis=1)
    my_q, their_q = columns(queries, group)
    my_g, their_g = columns(out_grad, group)
    q_rows = jnp.concatenate([my_q, swap_group(their_q)])
    g_rows = jnp.concatenate([my_g, swap_group(their_g)])
    pieces = gather_direct(blocks.reshape(PIECE, PAIR), "y")
    q_rows = gather_direct(q_rows, "x")
    across = jnp.concatenate(pieces)
    across, g_rows, *q_rows = lax.optimization_barrier((across, g_rows, *q_rows))
    pieces.append(swap_core(across))
    row_delta = jnp.sum(
        (wide(out_grad) * wide(outputs)).reshape(TOKENS, 2 * HEADS_HERE, HEAD_DIM), axis=2
    ).T.reshape(2, 1, ROWS)
    my_delta, their_delta = choose(row_delta[0], row_delta[1], group == 1)
    g_rows = gather_direct(g_rows, "x")
    delta = jnp.stack([my_delta, swap_group(their_delta)])

    stats = call_lse(tables, delta, q_rows, pieces)
    dq_pieces, d_pieces, d_other = call_grads(
        tables, q_rows, g_rows, gather_direct(stats, "x"), pieces
    )

    dq = reduce_direct(dq_pieces, "x")
    query_grad = jnp.concatenate(
        choose(dq[:TOKENS], swap_group(dq[TOKENS:]), group == 1), axis=1
    )

    arrived = swap_core(d_other)
    both = reduce_direct(
        [add(piece, arrived[i * PIECE : (i + 1) * PIECE]) for i, piece in enumerate(d_pieces)], "y"
    )
    both = both.reshape(4, 2, TOKENS, PAIR)
    kept, sent = choose(both[:, 0], both[:, 1], half == 1)
    near = add(kept, swap_half(sent))
    my_part = add(near[0], swap_z(near[2]))
    their_part = add(swap_group(near[1]), swap_both(near[3]))
    first, second = choose(my_part, their_part, group == 1)
    key_grad = jnp.concatenate([first[:, :HEAD_DIM], second[:, :HEAD_DIM]], axis=1)
    value_grad = jnp.concatenate([first[:, HEAD_DIM:], second[:, HEAD_DIM:]], axis=1)
    return query_grad, key_grad, value_grad


def solution(mesh):
    fine = Mesh(
        mesh.devices.reshape(4, 4, 2, 4, 2), ("head", "x", "zh", "y", "core")
    )
    rows = P(("x", "zh", "y", "core", "head"), None)
    return jax.shard_map(
        body,
        mesh=fine,
        in_specs=(rows, rows, rows, rows, rows, P()),
        out_specs=(rows, rows, rows),
        check_vma=False,
    )
```

```python
from functools import partial
import math

import jax
import jax.numpy as jnp
from jax import lax
from jax.experimental import pallas as pl
from jax.experimental.pallas import tpu as pltpu
from jax.sharding import Mesh, PartitionSpec as P

HEAD_DIM = 128
BLOCK = 128
TOKENS = 64
HEADS_HERE = 8
ROWS = TOKENS * HEADS_HERE
WIDE = HEADS_HERE * HEAD_DIM
CHUNK_BLOCKS = 4
CHUNK = CHUNK_BLOCKS * BLOCK
SLOTS = 32
TILES = 8
CHUNKS = SLOTS // CHUNK_BLOCKS
LOW_CHUNKS = CHUNKS // 2
UNITS = LOW_CHUNKS + 1
PIECE = 512
PIECES = 4
OTHER = PIECES * PIECE
PAIR = 2 * HEAD_DIM
OFFSETS = (0, -1, 1, 2)
PIECE_AT = {offset % 4: index for index, offset in enumerate(OFFSETS)}
FACTOR = HEAD_DIM ** (-0.5)
LOG2E = math.log2(math.e)
SCALE2 = FACTOR * LOG2E
NEG = -1e30
VMEM_BYTES = 48 * 1024 * 1024

def ring_pairs(steps):
    return [(source, (source + steps) % 4) for source in range(4)]


def send(value, axis, steps):
    return lax.ppermute(value, axis, ring_pairs(steps))


def swap_core(value):
    return lax.ppermute(value, "core", [(0, 1), (1, 0)])


def swap_group(value):
    return lax.ppermute(value, "head", [(source, source ^ 2) for source in range(4)])


def swap_half(value):
    return lax.ppermute(value, "head", [(source, source ^ 1) for source in range(4)])


def swap_z(value):
    return lax.ppermute(value, "zh", [(0, 1), (1, 0)])


def swap_both(value):
    return lax.ppermute(value, ("head", "zh"), [(source, source ^ 5) for source in range(8)])


def gather_direct(own, axis):
    return [own] + [send(own, axis, -offset) for offset in OFFSETS[1:]]


def wide(value):
    return value.astype(jnp.float32)


def add(*values):
    total = wide(values[0])
    for value in values[1:]:
        total = total + wide(value)
    return total.astype(jnp.bfloat16)


def reduce_direct(pieces, axis):
    arrived = [send(piece, axis, offset) for piece, offset in zip(pieces[1:], OFFSETS[1:])]
    return add(pieces[0], *arrived)


def kv_copies(pieces, other, gathered, sems, outward):
    copies = []
    for index in range(PIECES + 1):
        outside = other if index == PIECES else pieces[index]
        inside = gathered.at[pl.ds(index * PIECE, outside.shape[0])]
        ends = (inside, outside) if outward else (outside, inside)
        copy = pltpu.make_async_copy(*ends, sems.at[index])
        copy.start()
        copies.append(copy)
    return copies


def spread_heads(sources, target):
    for place, source in enumerate(sources):
        for kind in range(2):
            for head in range(HEADS_HERE):
                target[4 * kind + place, pl.ds(head * TOKENS, TOKENS), :] = source[
                    pl.ds(kind * TOKENS, TOKENS), pl.ds(head * HEAD_DIM, HEAD_DIM)
                ]


def load_chunk(source, slot_ref, chunk, column):
    return jnp.concatenate(
        [
            source[pl.ds(pl.multiple_of(slot_ref[chunk * CHUNK_BLOCKS + j] * BLOCK, BLOCK), BLOCK),
                pl.ds(column, HEAD_DIM),
            ]
            for j in range(CHUNK_BLOCKS)
        ],
        axis=0,
    )


def dot_rows(left, right):
    return lax.dot_general(
        left, right, (((1,), (1,)), ((), ())), preferred_element_type=jnp.float32
    )


def dot_columns(left, right):
    return lax.dot_general(
        left, right, (((0,), (0,)), ((), ())), preferred_element_type=jnp.float32
    )


def masked(value, fill, ids_ref, chunk, query_start):
    rows = lax.broadcasted_iota(jnp.int32, (BLOCK, ROWS), 0)
    lanes = lax.broadcasted_iota(jnp.int32, (BLOCK, ROWS), 1) % TOKENS
    ahead = rows - lanes
    parts = []
    for j in range(CHUNK_BLOCKS):
        limit = query_start - ids_ref[chunk * CHUNK_BLOCKS + j] * BLOCK
        parts.append(jnp.where(ahead <= limit, value[j * BLOCK : (j + 1) * BLOCK], fill))
    return jnp.concatenate(parts, axis=0)


def for_steps(unit_refs, step):
    tile_ref, chunk_ref, start_ref = unit_refs

    def high(chunk, carry):
        step([(4 + place, chunk, None) for place in range(4)])
        return carry

    def rest(index, carry):
        units = [4 * index + place for place in range(4)]
        step([(tile_ref[unit], chunk_ref[unit], start_ref[unit]) for unit in units])
        return carry

    lax.fori_loop(0, LOW_CHUNKS, high, 0)
    lax.fori_loop(0, UNITS, rest, 0)


def lse_kernel(slot_ref, ids_ref, tile_ref, chunk_ref, start_ref, delta_ref, *refs):
    rows, pieces, other = refs[:4], refs[4 : 4 + PIECES], refs[4 + PIECES]
    stat_ref, gathered, queries, max_acc, sum_acc, sems = refs[5 + PIECES :]
    copies = kv_copies(pieces, other, gathered, sems, False)
    spread_heads(rows, queries)
    max_acc[...] = jnp.full(max_acc.shape, NEG, jnp.float32)
    sum_acc[...] = jnp.zeros(sum_acc.shape, jnp.float32)
    for copy in copies:
        copy.wait()

    def step(units):
        scores = []
        for query, chunk, start in units:
            part = dot_rows(load_chunk(gathered, slot_ref, chunk, 0), queries[query])
            if start is not None:
                part = masked(part, NEG, ids_ref, chunk, start)
            scores.append(part.reshape(CHUNK // 8, 8, ROWS))
        for (query, _, _), part in zip(units, scores):
            old_max = max_acc[query]
            new_max = jnp.maximum(old_max, jnp.max(part, axis=0))
            weights = jnp.exp2((part - new_max[None]) * SCALE2)
            sum_acc[query] = sum_acc[query] * jnp.exp2((old_max - new_max) * SCALE2) + jnp.sum(
                weights, axis=0
            )
            max_acc[query] = new_max

    for_steps((tile_ref, chunk_ref, start_ref), step)
    for query in range(2):
        stat_ref[2 * TILES + query] = delta_ref[query]
    for query in range(TILES):
        part_max = max_acc[query]
        top = jnp.max(part_max, axis=0, keepdims=True)
        stat_ref[query] = top
        stat_ref[TILES + query] = jnp.sum(
            sum_acc[query] * jnp.exp2((part_max - top) * SCALE2), axis=0, keepdims=True
        )


def grad_kernel(slot_ref, ids_ref, tile_ref, chunk_ref, start_ref, *refs):
    q_rows, g_rows, stats = refs[:4], refs[4:8], refs[8:12]
    pieces, other = refs[12 : 12 + PIECES], refs[12 + PIECES]
    refs = refs[13 + PIECES :]
    dq_pieces, d_pieces, d_other = refs[:4], refs[4 : 4 + PIECES], refs[4 + PIECES]
    gathered, queries, grads, lse, delta, d_all, dk_acc, dv_acc, dq_acc, sems = refs[5 + PIECES :]
    copies = kv_copies(pieces, other, gathered, sems, False)
    spread_heads(q_rows, queries)
    spread_heads(g_rows, grads)
    for query in range(TILES):
        offset, kind = OFFSETS[query % 4], query // 4
        places = [4 * kind + PIECE_AT[(offset - source) % 4] for source in OFFSETS]
        tops = [stat[place] for stat, place in zip(stats, places)]
        top = jnp.maximum(jnp.maximum(tops[0], tops[1]), jnp.maximum(tops[2], tops[3]))
        total = jnp.zeros_like(top)
        for stat, place, part in zip(stats, places, tops):
            total += stat[TILES + place] * jnp.exp2((part - top) * SCALE2)
        lse[query] = top * SCALE2 + jnp.log2(total)
        delta[query] = stats[query % 4][2 * TILES + kind]
    dq_acc[...] = jnp.zeros(dq_acc.shape, jnp.float32)
    for copy in copies:
        copy.wait()

    for chunk in range(LOW_CHUNKS, CHUNKS):
        dk_acc[chunk] = jnp.zeros((CHUNK, HEAD_DIM), jnp.float32)
        dv_acc[chunk] = jnp.zeros((CHUNK, HEAD_DIM), jnp.float32)

    def high_step(chunk):
        key_part = load_chunk(gathered, slot_ref, chunk, 0)
        value_part = load_chunk(gathered, slot_ref, chunk, HEAD_DIM)
        query_part = queries[4:].reshape(4 * ROWS, HEAD_DIM)
        grad_part = grads[4:].reshape(4 * ROWS, HEAD_DIM)
        scores = dot_rows(key_part, query_part)
        dprob = dot_rows(value_part, grad_part)
        row_lse = jnp.concatenate([lse[4 + place] for place in range(4)], axis=1)
        row_delta = jnp.concatenate([delta[4 + place] for place in range(4)], axis=1)
        weights = jnp.exp2(scores * SCALE2 - row_lse)
        score_grad = (weights * (dprob - row_delta)).astype(jnp.bfloat16)
        dk_acc[chunk] = jnp.dot(score_grad, query_part, preferred_element_type=jnp.float32)
        dv_acc[chunk] = jnp.dot(
            weights.astype(jnp.bfloat16), grad_part, preferred_element_type=jnp.float32
        )
        dq = dot_columns(key_part, score_grad)
        for place in range(4):
            dq_acc[4 + place] += dq[:, place * ROWS : (place + 1) * ROWS]

    def products(query, chunk):
        key_part = load_chunk(gathered, slot_ref, chunk, 0)
        value_part = load_chunk(gathered, slot_ref, chunk, HEAD_DIM)
        return key_part, dot_rows(key_part, queries[query]), dot_rows(value_part, grads[query])

    def step(units):
        if units[0][2] is None:
            high_step(units[0][1])
            return
        parts = []
        ahead = products(*units[0][:2])
        for index, (query, chunk, start) in enumerate(units):
            key_part, scores, dprob = ahead
            if index + 1 < len(units):
                ahead = products(*units[index + 1][:2])
            weights = jnp.exp2(scores * SCALE2 - lse[query])
            weights = masked(weights, 0.0, ids_ref, chunk, start)
            score_grad = (weights * (dprob - delta[query])).astype(jnp.bfloat16)
            parts.append((
                dot_columns(key_part, score_grad),
                jnp.dot(score_grad, queries[query], preferred_element_type=jnp.float32),
                jnp.dot(
                    weights.astype(jnp.bfloat16),
                    grads[query],
                    preferred_element_type=jnp.float32,
                ),
            ))
        for (query, chunk, _), part in zip(units, parts):
            dq_acc[query] += part[0]
            dk_acc[chunk] += part[1]
            dv_acc[chunk] += part[2]

    for_steps((tile_ref, chunk_ref, start_ref), step)

    def place_chunk(chunk, carry):
        for j in range(CHUNK_BLOCKS):
            place = chunk * CHUNK_BLOCKS + j
            rows = pl.ds(j * BLOCK, BLOCK)
            target = pl.ds(pl.multiple_of(slot_ref[place] * BLOCK, BLOCK), BLOCK)
            d_all[target, pl.ds(0, HEAD_DIM)] = (dk_acc[chunk, rows, :] * FACTOR).astype(
                jnp.bfloat16
            )
            d_all[target, pl.ds(HEAD_DIM, HEAD_DIM)] = dv_acc[chunk, rows, :].astype(jnp.bfloat16)
        return carry

    lax.fori_loop(0, CHUNKS, place_chunk, 0)
    outs = kv_copies(d_pieces, d_other, d_all, sems, True)
    for query in range(TILES):
        target = dq_pieces[query % 4]
        for head in range(0, HEADS_HERE, 2):
            pair = (dq_acc[query, :, pl.ds(head * TOKENS, 2 * TOKENS)] * FACTOR).T
            for half in range(2):
                target[
                    pl.ds(query // 4 * TOKENS, TOKENS),
                    pl.ds((head + half) * HEAD_DIM, HEAD_DIM),
                ] = pair[half * TOKENS : (half + 1) * TOKENS].astype(target.dtype)
    for copy in outs:
        copy.wait()


SMEM = pl.BlockSpec(memory_space=pltpu.SMEM)
VMEM = pl.BlockSpec(memory_space=pltpu.VMEM)
ANY = pl.BlockSpec(memory_space=pl.ANY)
PAIRS = (SLOTS + 2) * TILES // 2


def call_lse(tables, delta, rows, pieces):
    work = PAIRS * BLOCK * ROWS
    return pl.pallas_call(
        lse_kernel,
        out_shape=jax.ShapeDtypeStruct((2 * TILES + 2, 1, ROWS), jnp.float32),
        in_specs=[SMEM] * 5 + [VMEM] * 5 + [ANY] * (PIECES + 1),
        out_specs=VMEM,
        scratch_shapes=[
            pltpu.VMEM((SLOTS * BLOCK, PAIR), jnp.bfloat16),
            pltpu.VMEM((TILES, ROWS, HEAD_DIM), jnp.bfloat16),
            pltpu.VMEM((TILES, 8, ROWS), jnp.float32),
            pltpu.VMEM((TILES, 8, ROWS), jnp.float32),
            pltpu.SemaphoreType.DMA((PIECES + 1,)),
        ],
        compiler_params=pltpu.CompilerParams(vmem_limit_bytes=VMEM_BYTES),
        cost_estimate=pl.CostEstimate(
            flops=8 * work * HEAD_DIM, bytes_accessed=4 << 20, transcendentals=work
        ),
        name="lse",
    )(*tables, delta, *rows, *pieces)


def call_grads(tables, q_rows, g_rows, stats, pieces):
    work = PAIRS * BLOCK * ROWS
    flat = jax.ShapeDtypeStruct((2 * TOKENS, WIDE), jnp.bfloat16)
    piece = jax.ShapeDtypeStruct((PIECE, PAIR), jnp.bfloat16)
    other = jax.ShapeDtypeStruct((OTHER, PAIR), jnp.bfloat16)
    results = pl.pallas_call(
        grad_kernel,
        out_shape=(flat,) * 4 + (piece,) * PIECES + (other,),
        in_specs=[SMEM] * 5 + [VMEM] * 12 + [ANY] * (PIECES + 1),
        out_specs=(VMEM,) * 4 + (ANY,) * (PIECES + 1),
        scratch_shapes=[
            pltpu.VMEM((SLOTS * BLOCK, PAIR), jnp.bfloat16),
            pltpu.VMEM((TILES, ROWS, HEAD_DIM), jnp.bfloat16),
            pltpu.VMEM((TILES, ROWS, HEAD_DIM), jnp.bfloat16),
            pltpu.VMEM((TILES, 1, ROWS), jnp.float32),
            pltpu.VMEM((TILES, 1, ROWS), jnp.float32),
            pltpu.VMEM((SLOTS * BLOCK, PAIR), jnp.bfloat16),
            pltpu.VMEM((CHUNKS, CHUNK, HEAD_DIM), jnp.float32),
            pltpu.VMEM((CHUNKS, CHUNK, HEAD_DIM), jnp.float32),
            pltpu.VMEM((TILES, HEAD_DIM, ROWS), jnp.float32),
            pltpu.SemaphoreType.DMA((PIECES + 1,)),
        ],
        compiler_params=pltpu.CompilerParams(vmem_limit_bytes=VMEM_BYTES),
        cost_estimate=pl.CostEstimate(
            flops=16 * work * HEAD_DIM, bytes_accessed=8 << 20, transcendentals=work
        ),
        name="grads",
    )(*tables, *q_rows, *g_rows, *stats, *pieces)
    return results[:4], results[4 : 4 + PIECES], results[4 + PIECES]


def lookup(table, wanted):
    places = jnp.arange(table.shape[0], dtype=jnp.int32)
    return jnp.sum(jnp.where(wanted[:, None] == places[None, :], table[None, :], 0), axis=1)


def plan(order):
    x, y, zh, core, head = (lax.axis_index(name) for name in ("x", "y", "zh", "core", "head"))
    group, half = head // 2, head % 2
    offsets = jnp.array(OFFSETS, jnp.int32)
    slot = jnp.arange(SLOTS, dtype=jnp.int32)
    piece, pair = slot // 4 % 4, slot % 4
    blk = (
        x * 16
        + (zh + pair // 2) % 2 * 8
        + (y + lookup(offsets, piece)) % 4 * 2
        + (core + slot // 16) % 2
    )
    ids = lookup(order, 2 * blk + (group + pair) % 2)
    tile = jnp.arange(TILES, dtype=jnp.int32)
    blk = (x + lookup(offsets, tile % 4)) % 4 * 16 + zh * 8 + y * 2 + core
    query_ids = lookup(order, 2 * blk + tile // 4)
    seen = jnp.sum((ids[None, :] <= query_ids[:, None]).astype(jnp.int32), axis=1)
    rank = jnp.sum((ids[None, :] < ids[:, None]).astype(jnp.int32), axis=1)
    hit = rank[None, :] == slot[:, None]
    slots = jnp.sum(jnp.where(hit, slot[None, :], 0), axis=1)
    sorted_ids = jnp.sum(jnp.where(hit, ids[None, :], 0), axis=1)
    chunks = (seen + CHUNK_BLOCKS - 1) // CHUNK_BLOCKS
    unit = jnp.arange(UNITS, dtype=jnp.int32)[:, None]
    place = jnp.arange(4, dtype=jnp.int32)[None, :]
    is_high = unit >= chunks[None, :4]
    later = LOW_CHUNKS + unit - chunks[None, :4]
    starts = query_ids * BLOCK + half * TOKENS
    left = jnp.where(later < chunks[None, 4:], starts[None, 4:], -BLOCK)
    unit_tiles = place + jnp.where(is_high, 4, 0)
    unit_chunks = jnp.where(is_high, jnp.minimum(later, CHUNKS - 1), unit)
    unit_starts = jnp.where(is_high, left, starts[None, :4])
    return (
        slots, sorted_ids, unit_tiles.reshape(-1), unit_chunks.reshape(-1), unit_starts.reshape(-1),
    )


def choose(first, second, swap):
    return jnp.where(swap, second, first), jnp.where(swap, first, second)


def columns(rows, group):
    width = rows.shape[1] // 2
    return choose(rows[:, :width], rows[:, width:], group == 1)


def body(queries, keys, values, outputs, out_grad, order):
    head = lax.axis_index("head")
    group, half = head // 2, head % 2
    tables = plan(order)

    my_keys, their_keys = columns(keys, group)
    my_values, their_values = columns(values, group)
    mine = jnp.concatenate([my_keys, my_values], axis=1)
    theirs = jnp.concatenate([their_keys, their_values], axis=1)
    near = jnp.stack([mine, swap_group(theirs), swap_z(mine), swap_both(theirs)])
    blocks = jnp.concatenate(choose(near, swap_half(near), half == 1), axis=1)
    my_q, their_q = columns(queries, group)
    my_g, their_g = columns(out_grad, group)
    q_rows = jnp.concatenate(choose(my_q, swap_group(their_q), group == 1))
    g_rows = jnp.concatenate(choose(my_g, swap_group(their_g), group == 1))
    pieces = gather_direct(blocks.reshape(PIECE, PAIR), "y")
    q_rows = gather_direct(q_rows, "x")
    across = jnp.concatenate(pieces)
    across, g_rows, *q_rows = lax.optimization_barrier((across, g_rows, *q_rows))
    pieces.append(swap_core(across))
    row_delta = jnp.sum(
        (wide(out_grad) * wide(outputs)).reshape(TOKENS, 2 * HEADS_HERE, HEAD_DIM), axis=2
    ).T.reshape(2, 1, ROWS)
    my_delta, their_delta = choose(row_delta[0], row_delta[1], group == 1)
    g_rows = gather_direct(g_rows, "x")
    delta = jnp.stack(choose(my_delta, swap_group(their_delta), group == 1))

    stats = call_lse(tables, delta, q_rows, pieces)
    dq_pieces, d_pieces, d_other = call_grads(
        tables, q_rows, g_rows, gather_direct(stats, "x"), pieces
    )

    dq = reduce_direct(dq_pieces, "x")
    my_dq, their_dq = choose(dq[:TOKENS], dq[TOKENS:], group == 1)
    query_grad = jnp.concatenate(choose(my_dq, swap_group(their_dq), group == 1), axis=1)

    arrived = swap_core(d_other)
    both = reduce_direct(
        [add(piece, arrived[i * PIECE : (i + 1) * PIECE]) for i, piece in enumerate(d_pieces)], "y"
    )
    both = both.reshape(4, 2, TOKENS, PAIR)
    kept, sent = choose(both[:, 0], both[:, 1], half == 1)
    near = add(kept, swap_half(sent))
    my_part = add(near[0], swap_z(near[2]))
    their_part = add(swap_group(near[1]), swap_both(near[3]))
    first, second = choose(my_part, their_part, group == 1)
    key_grad = jnp.concatenate([first[:, :HEAD_DIM], second[:, :HEAD_DIM]], axis=1)
    value_grad = jnp.concatenate([first[:, HEAD_DIM:], second[:, HEAD_DIM:]], axis=1)
    return query_grad, key_grad, value_grad


def solution(mesh):
    fine = Mesh(
        mesh.devices.reshape(4, 4, 2, 4, 2), ("head", "x", "zh", "y", "core")
    )
    rows = P(("x", "zh", "y", "core", "head"), None)
    return jax.shard_map(
        body,
        mesh=fine,
        in_specs=(rows, rows, rows, rows, rows, P()),
        out_specs=(rows, rows, rows),
        check_vma=False,
    )
```

```python
from functools import partial
import math

import jax
import jax.numpy as jnp
from jax import lax
from jax.experimental import pallas as pl
from jax.experimental.pallas import tpu as pltpu
from jax.sharding import Mesh, PartitionSpec as P

HEAD_DIM = 128
BLOCK = 128
TOKENS = 64
HEADS_HERE = 8
ROWS = TOKENS * HEADS_HERE
WIDE = HEADS_HERE * HEAD_DIM
CHUNK_BLOCKS = 4
CHUNK = CHUNK_BLOCKS * BLOCK
SLOTS = 32
TILES = 8
CHUNKS = SLOTS // CHUNK_BLOCKS
LOW_CHUNKS = CHUNKS // 2
UNITS = LOW_CHUNKS + 1
PIECE = 512
PIECES = 4
OTHER = PIECES * PIECE
PAIR = 2 * HEAD_DIM
OFFSETS = (0, -1, 1, 2)
PIECE_AT = {offset % 4: index for index, offset in enumerate(OFFSETS)}
FACTOR = HEAD_DIM ** (-0.5)
LOG2E = math.log2(math.e)
SCALE2 = FACTOR * LOG2E
NEG = -1e30
VMEM_BYTES = 48 * 1024 * 1024

def ring_pairs(steps):
    return [(source, (source + steps) % 4) for source in range(4)]


def send(value, axis, steps):
    return lax.ppermute(value, axis, ring_pairs(steps))


def swap_core(value):
    return lax.ppermute(value, "core", [(0, 1), (1, 0)])


def swap_group(value):
    return lax.ppermute(value, "head", [(source, source ^ 2) for source in range(4)])


def swap_half(value):
    return lax.ppermute(value, "head", [(source, source ^ 1) for source in range(4)])


def swap_z(value):
    return lax.ppermute(value, "zh", [(0, 1), (1, 0)])


def swap_both(value):
    return lax.ppermute(value, ("head", "zh"), [(source, source ^ 5) for source in range(8)])


def gather_direct(own, axis):
    return [own] + [send(own, axis, -offset) for offset in OFFSETS[1:]]


def wide(value):
    return value.astype(jnp.float32)


def add(*values):
    total = wide(values[0])
    for value in values[1:]:
        total = total + wide(value)
    return total.astype(jnp.bfloat16)


def reduce_direct(pieces, axis):
    arrived = [send(piece, axis, offset) for piece, offset in zip(pieces[1:], OFFSETS[1:])]
    return add(pieces[0], *arrived)


def reduce_ring(pieces, axis):
    own, left, right, far = pieces
    middle = far.shape[0] // 2
    from_right = send(far[:middle], axis, -1)
    from_left = send(far[middle:], axis, 1)
    left = jnp.concatenate([add(left[:middle], from_right), left[middle:]])
    right = jnp.concatenate([right[:middle], add(right[middle:], from_left)])
    return add(own, send(left, axis, -1), send(right, axis, 1))


def kv_copies(pieces, other, gathered, sems, outward):
    copies = []
    for index in range(PIECES + 1):
        outside = other if index == PIECES else pieces[index]
        inside = gathered.at[pl.ds(index * PIECE, outside.shape[0])]
        ends = (inside, outside) if outward else (outside, inside)
        copy = pltpu.make_async_copy(*ends, sems.at[index])
        copy.start()
        copies.append(copy)
    return copies


def spread_heads(sources, target):
    for place, source in enumerate(sources):
        for kind in range(2):
            for head in range(HEADS_HERE):
                target[4 * kind + place, pl.ds(head * TOKENS, TOKENS), :] = source[
                    pl.ds(kind * TOKENS, TOKENS), pl.ds(head * HEAD_DIM, HEAD_DIM)
                ]


def load_chunk(source, slot_ref, chunk, column):
    return jnp.concatenate(
        [
            source[pl.ds(pl.multiple_of(slot_ref[chunk * CHUNK_BLOCKS + j] * BLOCK, BLOCK), BLOCK),
                pl.ds(column, HEAD_DIM),
            ]
            for j in range(CHUNK_BLOCKS)
        ],
        axis=0,
    )


def dot_rows(left, right):
    return lax.dot_general(
        left, right, (((1,), (1,)), ((), ())), preferred_element_type=jnp.float32
    )


def dot_columns(left, right):
    return lax.dot_general(
        left, right, (((0,), (0,)), ((), ())), preferred_element_type=jnp.float32
    )


def masked(value, fill, ids_ref, chunk, query_start):
    rows = lax.broadcasted_iota(jnp.int32, (BLOCK, ROWS), 0)
    lanes = lax.broadcasted_iota(jnp.int32, (BLOCK, ROWS), 1) % TOKENS
    ahead = rows - lanes
    parts = []
    for j in range(CHUNK_BLOCKS):
        limit = query_start - ids_ref[chunk * CHUNK_BLOCKS + j] * BLOCK
        parts.append(jnp.where(ahead <= limit, value[j * BLOCK : (j + 1) * BLOCK], fill))
    return jnp.concatenate(parts, axis=0)


def for_steps(unit_refs, step):
    tile_ref, chunk_ref, start_ref = unit_refs

    def high(chunk, carry):
        step([(4 + place, chunk, None) for place in range(4)])
        return carry

    def rest(index, carry):
        units = [4 * index + place for place in range(4)]
        step([(tile_ref[unit], chunk_ref[unit], start_ref[unit]) for unit in units])
        return carry

    lax.fori_loop(0, LOW_CHUNKS, high, 0)
    lax.fori_loop(0, UNITS, rest, 0)


def lse_kernel(slot_ref, ids_ref, tile_ref, chunk_ref, start_ref, delta_ref, *refs):
    rows, pieces, other = refs[:4], refs[4 : 4 + PIECES], refs[4 + PIECES]
    stat_ref, gathered, queries, max_acc, sum_acc, sems = refs[5 + PIECES :]
    copies = kv_copies(pieces, other, gathered, sems, False)
    spread_heads(rows, queries)
    max_acc[...] = jnp.full(max_acc.shape, NEG, jnp.float32)
    sum_acc[...] = jnp.zeros(sum_acc.shape, jnp.float32)
    for copy in copies:
        copy.wait()

    def step(units):
        scores = []
        for query, chunk, start in units:
            part = dot_rows(load_chunk(gathered, slot_ref, chunk, 0), queries[query])
            if start is not None:
                part = masked(part, NEG, ids_ref, chunk, start)
            scores.append(part.reshape(CHUNK // 8, 8, ROWS))
        for (query, _, _), part in zip(units, scores):
            old_max = max_acc[query]
            new_max = jnp.maximum(old_max, jnp.max(part, axis=0))
            weights = jnp.exp2((part - new_max[None]) * SCALE2)
            sum_acc[query] = sum_acc[query] * jnp.exp2((old_max - new_max) * SCALE2) + jnp.sum(
                weights, axis=0
            )
            max_acc[query] = new_max

    for_steps((tile_ref, chunk_ref, start_ref), step)
    for query in range(2):
        stat_ref[2 * TILES + query] = delta_ref[query]
    for query in range(TILES):
        part_max = max_acc[query]
        top = jnp.max(part_max, axis=0, keepdims=True)
        stat_ref[query] = top
        stat_ref[TILES + query] = jnp.sum(
            sum_acc[query] * jnp.exp2((part_max - top) * SCALE2), axis=0, keepdims=True
        )


def grad_kernel(slot_ref, ids_ref, tile_ref, chunk_ref, start_ref, *refs):
    q_rows, g_rows, stats = refs[:4], refs[4:8], refs[8:12]
    pieces, other = refs[12 : 12 + PIECES], refs[12 + PIECES]
    refs = refs[13 + PIECES :]
    dq_pieces, d_pieces, d_other = refs[:4], refs[4 : 4 + PIECES], refs[4 + PIECES]
    gathered, queries, grads, lse, delta, d_all, dk_acc, dv_acc, dq_acc, sems = refs[5 + PIECES :]
    copies = kv_copies(pieces, other, gathered, sems, False)
    spread_heads(q_rows, queries)
    spread_heads(g_rows, grads)
    for query in range(TILES):
        offset, kind = OFFSETS[query % 4], query // 4
        places = [4 * kind + PIECE_AT[(offset - source) % 4] for source in OFFSETS]
        tops = [stat[place] for stat, place in zip(stats, places)]
        top = jnp.maximum(jnp.maximum(tops[0], tops[1]), jnp.maximum(tops[2], tops[3]))
        total = jnp.zeros_like(top)
        for stat, place, part in zip(stats, places, tops):
            total += stat[TILES + place] * jnp.exp2((part - top) * SCALE2)
        lse[query] = top * SCALE2 + jnp.log2(total)
        delta[query] = stats[query % 4][2 * TILES + kind]
    dq_acc[...] = jnp.zeros(dq_acc.shape, jnp.float32)
    for copy in copies:
        copy.wait()

    for chunk in range(LOW_CHUNKS, CHUNKS):
        dk_acc[chunk] = jnp.zeros((CHUNK, HEAD_DIM), jnp.float32)
        dv_acc[chunk] = jnp.zeros((CHUNK, HEAD_DIM), jnp.float32)

    def high_step(chunk):
        key_part = load_chunk(gathered, slot_ref, chunk, 0)
        value_part = load_chunk(gathered, slot_ref, chunk, HEAD_DIM)
        query_part = queries[4:].reshape(4 * ROWS, HEAD_DIM)
        grad_part = grads[4:].reshape(4 * ROWS, HEAD_DIM)
        scores = dot_rows(key_part, query_part)
        dprob = dot_rows(value_part, grad_part)
        row_lse = jnp.concatenate([lse[4 + place] for place in range(4)], axis=1)
        row_delta = jnp.concatenate([delta[4 + place] for place in range(4)], axis=1)
        weights = jnp.exp2(scores * SCALE2 - row_lse)
        score_grad = (weights * (dprob - row_delta)).astype(jnp.bfloat16)
        dk_acc[chunk] = jnp.dot(score_grad, query_part, preferred_element_type=jnp.float32)
        dv_acc[chunk] = jnp.dot(
            weights.astype(jnp.bfloat16), grad_part, preferred_element_type=jnp.float32
        )
        dq = dot_columns(key_part, score_grad)
        for place in range(4):
            dq_acc[4 + place] += dq[:, place * ROWS : (place + 1) * ROWS]

    def products(query, chunk):
        key_part = load_chunk(gathered, slot_ref, chunk, 0)
        value_part = load_chunk(gathered, slot_ref, chunk, HEAD_DIM)
        return key_part, dot_rows(key_part, queries[query]), dot_rows(value_part, grads[query])

    def step(units):
        if units[0][2] is None:
            high_step(units[0][1])
            return
        parts = []
        ahead = products(*units[0][:2])
        for index, (query, chunk, start) in enumerate(units):
            key_part, scores, dprob = ahead
            if index + 1 < len(units):
                ahead = products(*units[index + 1][:2])
            weights = jnp.exp2(scores * SCALE2 - lse[query])
            weights = masked(weights, 0.0, ids_ref, chunk, start)
            score_grad = (weights * (dprob - delta[query])).astype(jnp.bfloat16)
            parts.append((
                dot_columns(key_part, score_grad),
                jnp.dot(score_grad, queries[query], preferred_element_type=jnp.float32),
                jnp.dot(
                    weights.astype(jnp.bfloat16),
                    grads[query],
                    preferred_element_type=jnp.float32,
                ),
            ))
        for (query, chunk, _), part in zip(units, parts):
            dq_acc[query] += part[0]
            dk_acc[chunk] += part[1]
            dv_acc[chunk] += part[2]

    for_steps((tile_ref, chunk_ref, start_ref), step)

    def place_chunk(chunk, carry):
        for j in range(CHUNK_BLOCKS):
            place = chunk * CHUNK_BLOCKS + j
            rows = pl.ds(j * BLOCK, BLOCK)
            target = pl.ds(pl.multiple_of(slot_ref[place] * BLOCK, BLOCK), BLOCK)
            d_all[target, pl.ds(0, HEAD_DIM)] = (dk_acc[chunk, rows, :] * FACTOR).astype(
                jnp.bfloat16
            )
            d_all[target, pl.ds(HEAD_DIM, HEAD_DIM)] = dv_acc[chunk, rows, :].astype(jnp.bfloat16)
        return carry

    lax.fori_loop(0, CHUNKS, place_chunk, 0)
    outs = kv_copies(d_pieces, d_other, d_all, sems, True)
    for query in range(TILES):
        target = dq_pieces[query % 4]
        for head in range(0, HEADS_HERE, 2):
            pair = (dq_acc[query, :, pl.ds(head * TOKENS, 2 * TOKENS)] * FACTOR).T
            for half in range(2):
                target[
                    pl.ds(query // 4 * TOKENS, TOKENS),
                    pl.ds((head + half) * HEAD_DIM, HEAD_DIM),
                ] = pair[half * TOKENS : (half + 1) * TOKENS].astype(target.dtype)
    for copy in outs:
        copy.wait()


SMEM = pl.BlockSpec(memory_space=pltpu.SMEM)
VMEM = pl.BlockSpec(memory_space=pltpu.VMEM)
ANY = pl.BlockSpec(memory_space=pl.ANY)
PAIRS = (SLOTS + 2) * TILES // 2


def call_lse(tables, delta, rows, pieces):
    work = PAIRS * BLOCK * ROWS
    return pl.pallas_call(
        lse_kernel,
        out_shape=jax.ShapeDtypeStruct((2 * TILES + 2, 1, ROWS), jnp.float32),
        in_specs=[SMEM] * 5 + [VMEM] * 5 + [ANY] * (PIECES + 1),
        out_specs=VMEM,
        scratch_shapes=[
            pltpu.VMEM((SLOTS * BLOCK, PAIR), jnp.bfloat16),
            pltpu.VMEM((TILES, ROWS, HEAD_DIM), jnp.bfloat16),
            pltpu.VMEM((TILES, 8, ROWS), jnp.float32),
            pltpu.VMEM((TILES, 8, ROWS), jnp.float32),
            pltpu.SemaphoreType.DMA((PIECES + 1,)),
        ],
        compiler_params=pltpu.CompilerParams(vmem_limit_bytes=VMEM_BYTES),
        cost_estimate=pl.CostEstimate(
            flops=8 * work * HEAD_DIM, bytes_accessed=4 << 20, transcendentals=work
        ),
        name="lse",
    )(*tables, delta, *rows, *pieces)


def call_grads(tables, q_rows, g_rows, stats, pieces):
    work = PAIRS * BLOCK * ROWS
    flat = jax.ShapeDtypeStruct((2 * TOKENS, WIDE), jnp.bfloat16)
    piece = jax.ShapeDtypeStruct((PIECE, PAIR), jnp.bfloat16)
    other = jax.ShapeDtypeStruct((OTHER, PAIR), jnp.bfloat16)
    results = pl.pallas_call(
        grad_kernel,
        out_shape=(flat,) * 4 + (piece,) * PIECES + (other,),
        in_specs=[SMEM] * 5 + [VMEM] * 12 + [ANY] * (PIECES + 1),
        out_specs=(VMEM,) * 4 + (ANY,) * (PIECES + 1),
        scratch_shapes=[
            pltpu.VMEM((SLOTS * BLOCK, PAIR), jnp.bfloat16),
            pltpu.VMEM((TILES, ROWS, HEAD_DIM), jnp.bfloat16),
            pltpu.VMEM((TILES, ROWS, HEAD_DIM), jnp.bfloat16),
            pltpu.VMEM((TILES, 1, ROWS), jnp.float32),
            pltpu.VMEM((TILES, 1, ROWS), jnp.float32),
            pltpu.VMEM((SLOTS * BLOCK, PAIR), jnp.bfloat16),
            pltpu.VMEM((CHUNKS, CHUNK, HEAD_DIM), jnp.float32),
            pltpu.VMEM((CHUNKS, CHUNK, HEAD_DIM), jnp.float32),
            pltpu.VMEM((TILES, HEAD_DIM, ROWS), jnp.float32),
            pltpu.SemaphoreType.DMA((PIECES + 1,)),
        ],
        compiler_params=pltpu.CompilerParams(vmem_limit_bytes=VMEM_BYTES),
        cost_estimate=pl.CostEstimate(
            flops=16 * work * HEAD_DIM, bytes_accessed=8 << 20, transcendentals=work
        ),
        name="grads",
    )(*tables, *q_rows, *g_rows, *stats, *pieces)
    return results[:4], results[4 : 4 + PIECES], results[4 + PIECES]


def lookup(table, wanted):
    places = jnp.arange(table.shape[0], dtype=jnp.int32)
    return jnp.sum(jnp.where(wanted[:, None] == places[None, :], table[None, :], 0), axis=1)


def plan(order):
    x, y, zh, core, head = (lax.axis_index(name) for name in ("x", "y", "zh", "core", "head"))
    group, half = head // 2, head % 2
    offsets = jnp.array(OFFSETS, jnp.int32)
    slot = jnp.arange(SLOTS, dtype=jnp.int32)
    piece, pair = slot // 4 % 4, slot % 4
    blk = (
        x * 16
        + (zh + pair // 2) % 2 * 8
        + (y + lookup(offsets, piece)) % 4 * 2
        + (core + slot // 16) % 2
    )
    ids = lookup(order, 2 * blk + (group + pair) % 2)
    tile = jnp.arange(TILES, dtype=jnp.int32)
    blk = (x + lookup(offsets, tile % 4)) % 4 * 16 + zh * 8 + y * 2 + core
    query_ids = lookup(order, 2 * blk + tile // 4)
    seen = jnp.sum((ids[None, :] <= query_ids[:, None]).astype(jnp.int32), axis=1)
    rank = jnp.sum((ids[None, :] < ids[:, None]).astype(jnp.int32), axis=1)
    hit = rank[None, :] == slot[:, None]
    slots = jnp.sum(jnp.where(hit, slot[None, :], 0), axis=1)
    sorted_ids = jnp.sum(jnp.where(hit, ids[None, :], 0), axis=1)
    chunks = (seen + CHUNK_BLOCKS - 1) // CHUNK_BLOCKS
    unit = jnp.arange(UNITS, dtype=jnp.int32)[:, None]
    place = jnp.arange(4, dtype=jnp.int32)[None, :]
    is_high = unit >= chunks[None, :4]
    later = LOW_CHUNKS + unit - chunks[None, :4]
    starts = query_ids * BLOCK + half * TOKENS
    left = jnp.where(later < chunks[None, 4:], starts[None, 4:], -BLOCK)
    unit_tiles = place + jnp.where(is_high, 4, 0)
    unit_chunks = jnp.where(is_high, jnp.minimum(later, CHUNKS - 1), unit)
    unit_starts = jnp.where(is_high, left, starts[None, :4])
    return (
        slots, sorted_ids, unit_tiles.reshape(-1), unit_chunks.reshape(-1), unit_starts.reshape(-1),
    )


def choose(first, second, swap):
    return jnp.where(swap, second, first), jnp.where(swap, first, second)


def columns(rows, group):
    width = rows.shape[1] // 2
    return choose(rows[:, :width], rows[:, width:], group == 1)


def body(queries, keys, values, outputs, out_grad, order):
    head = lax.axis_index("head")
    group, half = head // 2, head % 2
    tables = plan(order)

    my_keys, their_keys = columns(keys, group)
    my_values, their_values = columns(values, group)
    mine = jnp.concatenate([my_keys, my_values], axis=1)
    theirs = jnp.concatenate([their_keys, their_values], axis=1)
    near = [mine, swap_group(theirs), swap_z(mine), swap_both(theirs)]
    my_g, their_g = columns(out_grad, group)
    their_g, *near = lax.optimization_barrier((their_g, *near))
    near = jnp.stack(near)
    blocks = jnp.concatenate(choose(near, swap_half(near), half == 1), axis=1)
    my_q, their_q = columns(queries, group)
    q_rows = jnp.concatenate(choose(my_q, swap_group(their_q), group == 1))
    g_rows = jnp.concatenate(choose(my_g, swap_group(their_g), group == 1))
    pieces = gather_direct(blocks.reshape(PIECE, PAIR), "y")
    q_rows = gather_direct(q_rows, "x")
    across = jnp.concatenate(pieces)
    across, g_rows, *q_rows = lax.optimization_barrier((across, g_rows, *q_rows))
    pieces.append(swap_core(across))
    row_delta = jnp.sum(
        (wide(out_grad) * wide(outputs)).reshape(TOKENS, 2 * HEADS_HERE, HEAD_DIM), axis=2
    ).T.reshape(2, 1, ROWS)
    my_delta, their_delta = choose(row_delta[0], row_delta[1], group == 1)
    g_rows = gather_direct(g_rows, "x")
    delta = jnp.stack(choose(my_delta, swap_group(their_delta), group == 1))

    stats = call_lse(tables, delta, q_rows, pieces)
    dq_pieces, d_pieces, d_other = call_grads(
        tables, q_rows, g_rows, gather_direct(stats, "x"), pieces
    )

    dq = reduce_direct(dq_pieces, "x")
    my_dq, their_dq = choose(dq[:TOKENS], dq[TOKENS:], group == 1)
    query_grad = jnp.concatenate(choose(my_dq, swap_group(their_dq), group == 1), axis=1)

    arrived = swap_core(d_other)
    both = reduce_ring(
        [add(piece, arrived[i * PIECE : (i + 1) * PIECE]) for i, piece in enumerate(d_pieces)], "y"
    )
    both = both.reshape(4, 2, TOKENS, PAIR)
    kept, sent = choose(both[:, 0], both[:, 1], half == 1)
    near = add(kept, swap_half(sent))
    my_part = add(near[0], swap_z(near[2]))
    their_part = add(swap_group(near[1]), swap_both(near[3]))
    first, second = choose(my_part, their_part, group == 1)
    key_grad = jnp.concatenate([first[:, :HEAD_DIM], second[:, :HEAD_DIM]], axis=1)
    value_grad = jnp.concatenate([first[:, HEAD_DIM:], second[:, HEAD_DIM:]], axis=1)
    return query_grad, key_grad, value_grad


def solution(mesh):
    fine = Mesh(
        mesh.devices.reshape(4, 4, 2, 4, 2), ("head", "x", "zh", "y", "core")
    )
    rows = P(("x", "zh", "y", "core", "head"), None)
    return jax.shard_map(
        body,
        mesh=fine,
        in_specs=(rows, rows, rows, rows, rows, P()),
        out_specs=(rows, rows, rows),
        check_vma=False,
    )
```

```python
from functools import partial
import math

import jax
import jax.numpy as jnp
from jax import lax
from jax.experimental import pallas as pl
from jax.experimental.pallas import tpu as pltpu
from jax.sharding import Mesh, PartitionSpec as P

HEAD_DIM = 128
BLOCK = 128
TOKENS = 64
HEADS_HERE = 8
ROWS = TOKENS * HEADS_HERE
WIDE = HEADS_HERE * HEAD_DIM
CHUNK_BLOCKS = 4
CHUNK = CHUNK_BLOCKS * BLOCK
SLOTS = 32
TILES = 8
CHUNKS = SLOTS // CHUNK_BLOCKS
LOW_CHUNKS = CHUNKS // 2
UNITS = LOW_CHUNKS + 1
PIECE = 512
PIECES = 4
OTHER = PIECES * PIECE
PAIR = 2 * HEAD_DIM
OFFSETS = (0, -1, 1, 2)
PIECE_AT = {offset % 4: index for index, offset in enumerate(OFFSETS)}
FACTOR = HEAD_DIM ** (-0.5)
LOG2E = math.log2(math.e)
SCALE2 = FACTOR * LOG2E
NEG = -1e30
VMEM_BYTES = 48 * 1024 * 1024

def ring_pairs(steps):
    return [(source, (source + steps) % 4) for source in range(4)]


def send(value, axis, steps):
    return lax.ppermute(value, axis, ring_pairs(steps))


def swap_core(value):
    return lax.ppermute(value, "core", [(0, 1), (1, 0)])


def swap_group(value):
    return lax.ppermute(value, "head", [(source, source ^ 2) for source in range(4)])


def swap_half(value):
    return lax.ppermute(value, "head", [(source, source ^ 1) for source in range(4)])


def swap_z(value):
    return lax.ppermute(value, "zh", [(0, 1), (1, 0)])


def swap_both(value):
    return lax.ppermute(value, ("head", "zh"), [(source, source ^ 5) for source in range(8)])


def gather_direct(own, axis):
    return [own] + [send(own, axis, -offset) for offset in OFFSETS[1:]]


def wide(value):
    return value.astype(jnp.float32)


def add(*values):
    total = wide(values[0])
    for value in values[1:]:
        total = total + wide(value)
    return total.astype(jnp.bfloat16)


def reduce_direct(pieces, axis):
    arrived = [send(piece, axis, offset) for piece, offset in zip(pieces[1:], OFFSETS[1:])]
    return add(pieces[0], *arrived)


def reduce_ring(pieces, axis):
    own, left, right, far = pieces
    middle = far.shape[0] // 2
    from_right = send(far[:middle], axis, -1)
    from_left = send(far[middle:], axis, 1)
    left = jnp.concatenate([add(left[:middle], from_right), left[middle:]])
    right = jnp.concatenate([right[:middle], add(right[middle:], from_left)])
    return add(own, send(left, axis, -1), send(right, axis, 1))


def kv_copies(pieces, other, gathered, sems, outward):
    copies = []
    for index in range(PIECES + 1):
        outside = other if index == PIECES else pieces[index]
        inside = gathered.at[pl.ds(index * PIECE, outside.shape[0])]
        ends = (inside, outside) if outward else (outside, inside)
        copy = pltpu.make_async_copy(*ends, sems.at[index])
        copy.start()
        copies.append(copy)
    return copies


def spread_heads(sources, target):
    for place, source in enumerate(sources):
        for kind in range(2):
            for head in range(HEADS_HERE):
                target[4 * kind + place, pl.ds(head * TOKENS, TOKENS), :] = source[
                    pl.ds(kind * TOKENS, TOKENS), pl.ds(head * HEAD_DIM, HEAD_DIM)
                ]


def load_chunk(source, slot_ref, chunk, column):
    return jnp.concatenate(
        [
            source[pl.ds(pl.multiple_of(slot_ref[chunk * CHUNK_BLOCKS + j] * BLOCK, BLOCK), BLOCK),
                pl.ds(column, HEAD_DIM),
            ]
            for j in range(CHUNK_BLOCKS)
        ],
        axis=0,
    )


def dot_rows(left, right):
    return lax.dot_general(
        left, right, (((1,), (1,)), ((), ())), preferred_element_type=jnp.float32
    )


def dot_columns(left, right):
    return lax.dot_general(
        left, right, (((0,), (0,)), ((), ())), preferred_element_type=jnp.float32
    )


def masked(value, fill, ids_ref, chunk, query_start):
    rows = lax.broadcasted_iota(jnp.int32, (BLOCK, ROWS), 0)
    lanes = lax.broadcasted_iota(jnp.int32, (BLOCK, ROWS), 1) % TOKENS
    ahead = rows - lanes
    parts = []
    for j in range(CHUNK_BLOCKS):
        limit = query_start - ids_ref[chunk * CHUNK_BLOCKS + j] * BLOCK
        parts.append(jnp.where(ahead <= limit, value[j * BLOCK : (j + 1) * BLOCK], fill))
    return jnp.concatenate(parts, axis=0)


def for_steps(unit_refs, step):
    tile_ref, chunk_ref, start_ref = unit_refs

    def high(chunk, carry):
        step([(4 + place, chunk, None) for place in range(4)])
        return carry

    def rest(index, carry):
        units = [4 * index + place for place in range(4)]
        step([(tile_ref[unit], chunk_ref[unit], start_ref[unit]) for unit in units])
        return carry

    lax.fori_loop(0, LOW_CHUNKS, high, 0)
    lax.fori_loop(0, UNITS, rest, 0)


def lse_kernel(slot_ref, ids_ref, tile_ref, chunk_ref, start_ref, delta_ref, *refs):
    rows, pieces, other = refs[:4], refs[4 : 4 + PIECES], refs[4 + PIECES]
    stat_ref, gathered, queries, max_acc, sum_acc, sems = refs[5 + PIECES :]
    copies = kv_copies(pieces, other, gathered, sems, False)
    spread_heads(rows, queries)
    max_acc[...] = jnp.full(max_acc.shape, NEG, jnp.float32)
    sum_acc[...] = jnp.zeros(sum_acc.shape, jnp.float32)
    for copy in copies:
        copy.wait()

    def step(units):
        scores = []
        for query, chunk, start in units:
            part = dot_rows(load_chunk(gathered, slot_ref, chunk, 0), queries[query])
            if start is not None:
                part = masked(part, NEG, ids_ref, chunk, start)
            scores.append(part.reshape(CHUNK // 8, 8, ROWS))
        for (query, _, _), part in zip(units, scores):
            old_max = max_acc[query]
            new_max = jnp.maximum(old_max, jnp.max(part, axis=0))
            weights = jnp.exp2((part - new_max[None]) * SCALE2)
            sum_acc[query] = sum_acc[query] * jnp.exp2((old_max - new_max) * SCALE2) + jnp.sum(
                weights, axis=0
            )
            max_acc[query] = new_max

    for_steps((tile_ref, chunk_ref, start_ref), step)
    for query in range(2):
        stat_ref[2 * TILES + query] = delta_ref[query]
    for query in range(TILES):
        part_max = max_acc[query]
        top = jnp.max(part_max, axis=0, keepdims=True)
        stat_ref[query] = top
        stat_ref[TILES + query] = jnp.sum(
            sum_acc[query] * jnp.exp2((part_max - top) * SCALE2), axis=0, keepdims=True
        )


def grad_kernel(slot_ref, ids_ref, tile_ref, chunk_ref, start_ref, *refs):
    q_rows, g_rows, stats = refs[:4], refs[4:8], refs[8:12]
    pieces, other = refs[12 : 12 + PIECES], refs[12 + PIECES]
    refs = refs[13 + PIECES :]
    dq_pieces, d_pieces, d_other = refs[:4], refs[4 : 4 + PIECES], refs[4 + PIECES]
    gathered, queries, grads, lse, delta, d_all, dk_acc, dv_acc, dq_acc, sems = refs[5 + PIECES :]
    copies = kv_copies(pieces, other, gathered, sems, False)
    spread_heads(q_rows, queries)
    spread_heads(g_rows, grads)
    for query in range(TILES):
        offset, kind = OFFSETS[query % 4], query // 4
        places = [4 * kind + PIECE_AT[(offset - source) % 4] for source in OFFSETS]
        tops = [stat[place] for stat, place in zip(stats, places)]
        top = jnp.maximum(jnp.maximum(tops[0], tops[1]), jnp.maximum(tops[2], tops[3]))
        total = jnp.zeros_like(top)
        for stat, place, part in zip(stats, places, tops):
            total += stat[TILES + place] * jnp.exp2((part - top) * SCALE2)
        lse[query] = top * SCALE2 + jnp.log2(total)
        delta[query] = stats[query % 4][2 * TILES + kind]
    dq_acc[...] = jnp.zeros(dq_acc.shape, jnp.float32)
    for copy in copies:
        copy.wait()

    for chunk in range(LOW_CHUNKS, CHUNKS):
        dk_acc[chunk] = jnp.zeros((CHUNK, HEAD_DIM), jnp.float32)
        dv_acc[chunk] = jnp.zeros((CHUNK, HEAD_DIM), jnp.float32)

    def high_step(chunk):
        key_part = load_chunk(gathered, slot_ref, chunk, 0)
        value_part = load_chunk(gathered, slot_ref, chunk, HEAD_DIM)
        query_part = queries[4:].reshape(4 * ROWS, HEAD_DIM)
        grad_part = grads[4:].reshape(4 * ROWS, HEAD_DIM)
        scores = dot_rows(key_part, query_part)
        dprob = dot_rows(value_part, grad_part)
        row_lse = jnp.concatenate([lse[4 + place] for place in range(4)], axis=1)
        row_delta = jnp.concatenate([delta[4 + place] for place in range(4)], axis=1)
        weights = jnp.exp2(scores * SCALE2 - row_lse)
        score_grad = (weights * (dprob - row_delta)).astype(jnp.bfloat16)
        dk_acc[chunk] = jnp.dot(score_grad, query_part, preferred_element_type=jnp.float32)
        dv_acc[chunk] = jnp.dot(
            weights.astype(jnp.bfloat16), grad_part, preferred_element_type=jnp.float32
        )
        dq = dot_columns(key_part, score_grad)
        for place in range(4):
            dq_acc[4 + place] += dq[:, place * ROWS : (place + 1) * ROWS]

    def products(query, chunk):
        key_part = load_chunk(gathered, slot_ref, chunk, 0)
        value_part = load_chunk(gathered, slot_ref, chunk, HEAD_DIM)
        return key_part, dot_rows(key_part, queries[query]), dot_rows(value_part, grads[query])

    def step(units):
        if units[0][2] is None:
            high_step(units[0][1])
            return
        parts = []
        ahead = products(*units[0][:2])
        for index, (query, chunk, start) in enumerate(units):
            key_part, scores, dprob = ahead
            if index + 1 < len(units):
                ahead = products(*units[index + 1][:2])
            weights = jnp.exp2(scores * SCALE2 - lse[query])
            weights = masked(weights, 0.0, ids_ref, chunk, start)
            score_grad = (weights * (dprob - delta[query])).astype(jnp.bfloat16)
            parts.append((
                dot_columns(key_part, score_grad),
                jnp.dot(score_grad, queries[query], preferred_element_type=jnp.float32),
                jnp.dot(
                    weights.astype(jnp.bfloat16),
                    grads[query],
                    preferred_element_type=jnp.float32,
                ),
            ))
        for (query, chunk, _), part in zip(units, parts):
            dq_acc[query] += part[0]
            dk_acc[chunk] += part[1]
            dv_acc[chunk] += part[2]

    for_steps((tile_ref, chunk_ref, start_ref), step)

    def place_chunk(chunk, carry):
        for j in range(CHUNK_BLOCKS):
            place = chunk * CHUNK_BLOCKS + j
            rows = pl.ds(j * BLOCK, BLOCK)
            target = pl.ds(pl.multiple_of(slot_ref[place] * BLOCK, BLOCK), BLOCK)
            d_all[target, pl.ds(0, HEAD_DIM)] = (dk_acc[chunk, rows, :] * FACTOR).astype(
                jnp.bfloat16
            )
            d_all[target, pl.ds(HEAD_DIM, HEAD_DIM)] = dv_acc[chunk, rows, :].astype(jnp.bfloat16)
        return carry

    lax.fori_loop(0, CHUNKS, place_chunk, 0)
    outs = kv_copies(d_pieces, d_other, d_all, sems, True)
    for query in range(TILES):
        target = dq_pieces[query % 4]
        for head in range(0, HEADS_HERE, 2):
            pair = (dq_acc[query, :, pl.ds(head * TOKENS, 2 * TOKENS)] * FACTOR).T
            for half in range(2):
                target[
                    pl.ds(query // 4 * TOKENS, TOKENS),
                    pl.ds((head + half) * HEAD_DIM, HEAD_DIM),
                ] = pair[half * TOKENS : (half + 1) * TOKENS].astype(target.dtype)
    for copy in outs:
        copy.wait()


SMEM = pl.BlockSpec(memory_space=pltpu.SMEM)
VMEM = pl.BlockSpec(memory_space=pltpu.VMEM)
ANY = pl.BlockSpec(memory_space=pl.ANY)
PAIRS = (SLOTS + 2) * TILES // 2


def call_lse(tables, delta, rows, pieces):
    work = PAIRS * BLOCK * ROWS
    return pl.pallas_call(
        lse_kernel,
        out_shape=jax.ShapeDtypeStruct((2 * TILES + 2, 1, ROWS), jnp.float32),
        in_specs=[SMEM] * 5 + [VMEM] * 5 + [ANY] * (PIECES + 1),
        out_specs=VMEM,
        scratch_shapes=[
            pltpu.VMEM((SLOTS * BLOCK, PAIR), jnp.bfloat16),
            pltpu.VMEM((TILES, ROWS, HEAD_DIM), jnp.bfloat16),
            pltpu.VMEM((TILES, 8, ROWS), jnp.float32),
            pltpu.VMEM((TILES, 8, ROWS), jnp.float32),
            pltpu.SemaphoreType.DMA((PIECES + 1,)),
        ],
        compiler_params=pltpu.CompilerParams(vmem_limit_bytes=VMEM_BYTES),
        cost_estimate=pl.CostEstimate(
            flops=8 * work * HEAD_DIM, bytes_accessed=4 << 20, transcendentals=work
        ),
        name="lse",
    )(*tables, delta, *rows, *pieces)


def call_grads(tables, q_rows, g_rows, stats, pieces):
    work = PAIRS * BLOCK * ROWS
    flat = jax.ShapeDtypeStruct((2 * TOKENS, WIDE), jnp.bfloat16)
    piece = jax.ShapeDtypeStruct((PIECE, PAIR), jnp.bfloat16)
    other = jax.ShapeDtypeStruct((OTHER, PAIR), jnp.bfloat16)
    results = pl.pallas_call(
        grad_kernel,
        out_shape=(flat,) * 4 + (piece,) * PIECES + (other,),
        in_specs=[SMEM] * 5 + [VMEM] * 12 + [ANY] * (PIECES + 1),
        out_specs=(VMEM,) * 4 + (ANY,) * (PIECES + 1),
        scratch_shapes=[
            pltpu.VMEM((SLOTS * BLOCK, PAIR), jnp.bfloat16),
            pltpu.VMEM((TILES, ROWS, HEAD_DIM), jnp.bfloat16),
            pltpu.VMEM((TILES, ROWS, HEAD_DIM), jnp.bfloat16),
            pltpu.VMEM((TILES, 1, ROWS), jnp.float32),
            pltpu.VMEM((TILES, 1, ROWS), jnp.float32),
            pltpu.VMEM((SLOTS * BLOCK, PAIR), jnp.bfloat16),
            pltpu.VMEM((CHUNKS, CHUNK, HEAD_DIM), jnp.float32),
            pltpu.VMEM((CHUNKS, CHUNK, HEAD_DIM), jnp.float32),
            pltpu.VMEM((TILES, HEAD_DIM, ROWS), jnp.float32),
            pltpu.SemaphoreType.DMA((PIECES + 1,)),
        ],
        compiler_params=pltpu.CompilerParams(vmem_limit_bytes=VMEM_BYTES),
        cost_estimate=pl.CostEstimate(
            flops=16 * work * HEAD_DIM, bytes_accessed=8 << 20, transcendentals=work
        ),
        name="grads",
    )(*tables, *q_rows, *g_rows, *stats, *pieces)
    return results[:4], results[4 : 4 + PIECES], results[4 + PIECES]


def lookup(table, wanted):
    places = jnp.arange(table.shape[0], dtype=jnp.int32)
    return jnp.sum(jnp.where(wanted[:, None] == places[None, :], table[None, :], 0), axis=1)


def plan(order):
    x, y, zh, core, head = (lax.axis_index(name) for name in ("x", "y", "zh", "core", "head"))
    group, half = head // 2, head % 2
    offsets = jnp.array(OFFSETS, jnp.int32)
    slot = jnp.arange(SLOTS, dtype=jnp.int32)
    piece, pair = slot // 4 % 4, slot % 4
    blk = (
        x * 16
        + (zh + pair // 2) % 2 * 8
        + (y + lookup(offsets, piece)) % 4 * 2
        + (core + slot // 16) % 2
    )
    ids = lookup(order, 2 * blk + (group + pair) % 2)
    tile = jnp.arange(TILES, dtype=jnp.int32)
    blk = (x + lookup(offsets, tile % 4)) % 4 * 16 + zh * 8 + y * 2 + core
    query_ids = lookup(order, 2 * blk + tile // 4)
    seen = jnp.sum((ids[None, :] <= query_ids[:, None]).astype(jnp.int32), axis=1)
    rank = jnp.sum((ids[None, :] < ids[:, None]).astype(jnp.int32), axis=1)
    hit = rank[None, :] == slot[:, None]
    slots = jnp.sum(jnp.where(hit, slot[None, :], 0), axis=1)
    sorted_ids = jnp.sum(jnp.where(hit, ids[None, :], 0), axis=1)
    chunks = (seen + CHUNK_BLOCKS - 1) // CHUNK_BLOCKS
    unit = jnp.arange(UNITS, dtype=jnp.int32)[:, None]
    place = jnp.arange(4, dtype=jnp.int32)[None, :]
    is_high = unit >= chunks[None, :4]
    later = LOW_CHUNKS + unit - chunks[None, :4]
    starts = query_ids * BLOCK + half * TOKENS
    left = jnp.where(later < chunks[None, 4:], starts[None, 4:], -BLOCK)
    unit_tiles = place + jnp.where(is_high, 4, 0)
    unit_chunks = jnp.where(is_high, jnp.minimum(later, CHUNKS - 1), unit)
    unit_starts = jnp.where(is_high, left, starts[None, :4])
    return (
        slots, sorted_ids, unit_tiles.reshape(-1), unit_chunks.reshape(-1), unit_starts.reshape(-1),
    )


def choose(first, second, swap):
    return jnp.where(swap, second, first), jnp.where(swap, first, second)


def columns(rows, group):
    width = rows.shape[1] // 2
    return choose(rows[:, :width], rows[:, width:], group == 1)


def body(queries, keys, values, outputs, out_grad, order):
    head = lax.axis_index("head")
    group, half = head // 2, head % 2
    tables = plan(order)

    my_keys, their_keys = columns(keys, group)
    my_values, their_values = columns(values, group)
    mine = jnp.concatenate([my_keys, my_values], axis=1)
    theirs = jnp.concatenate([their_keys, their_values], axis=1)
    near = [mine, swap_group(theirs), swap_z(mine), swap_both(theirs)]
    my_g, their_g = columns(out_grad, group)
    their_g, *near = lax.optimization_barrier((their_g, *near))
    near = jnp.stack(near)
    blocks = jnp.concatenate(choose(near, swap_half(near), half == 1), axis=1)
    my_q, their_q = columns(queries, group)
    q_rows = jnp.concatenate(choose(my_q, swap_group(their_q), group == 1))
    g_rows = jnp.concatenate(choose(my_g, swap_group(their_g), group == 1))
    pieces = gather_direct(blocks.reshape(PIECE, PAIR), "y")
    q_rows = gather_direct(q_rows, "x")
    across = jnp.concatenate(pieces)
    g_rows, q_rows[1] = lax.optimization_barrier((g_rows, q_rows[1]))
    across, *q_rows = lax.optimization_barrier((across, *q_rows))
    pieces.append(swap_core(across))
    row_delta = jnp.sum(
        (wide(out_grad) * wide(outputs)).reshape(TOKENS, 2 * HEADS_HERE, HEAD_DIM), axis=2
    ).T.reshape(2, 1, ROWS)
    my_delta, their_delta = choose(row_delta[0], row_delta[1], group == 1)
    g_rows = gather_direct(g_rows, "x")
    delta = jnp.stack(choose(my_delta, swap_group(their_delta), group == 1))

    stats = call_lse(tables, delta, q_rows, pieces)
    dq_pieces, d_pieces, d_other = call_grads(
        tables, q_rows, g_rows, gather_direct(stats, "x"), pieces
    )

    dq = reduce_direct(dq_pieces, "x")
    my_dq, their_dq = choose(dq[:TOKENS], dq[TOKENS:], group == 1)
    query_grad = jnp.concatenate(choose(my_dq, swap_group(their_dq), group == 1), axis=1)

    arrived = swap_core(d_other)
    both = reduce_ring(
        [add(piece, arrived[i * PIECE : (i + 1) * PIECE]) for i, piece in enumerate(d_pieces)], "y"
    )
    both = both.reshape(4, 2, TOKENS, PAIR)
    kept, sent = choose(both[:, 0], both[:, 1], half == 1)
    near = add(kept, swap_half(sent))
    my_part = add(near[0], swap_z(near[2]))
    their_part = add(swap_group(near[1]), swap_both(near[3]))
    first, second = choose(my_part, their_part, group == 1)
    key_grad = jnp.concatenate([first[:, :HEAD_DIM], second[:, :HEAD_DIM]], axis=1)
    value_grad = jnp.concatenate([first[:, HEAD_DIM:], second[:, HEAD_DIM:]], axis=1)
    return query_grad, key_grad, value_grad


def solution(mesh):
    fine = Mesh(
        mesh.devices.reshape(4, 4, 2, 4, 2), ("head", "x", "zh", "y", "core")
    )
    rows = P(("x", "zh", "y", "core", "head"), None)
    return jax.shard_map(
        body,
        mesh=fine,
        in_specs=(rows, rows, rows, rows, rows, P()),
        out_specs=(rows, rows, rows),
        check_vma=False,
    )
```
